128 devices in a mesh: dom: 128 (over x, y, z, core).
Axes of the slice: x: 4, y: 4, z: 4, core: 2. Of those that a mesh axis runs over, the one named last changes fastest.
Arguments:
- state: float32 [5, 125, 32768], P(None, None, 'dom'), may hold values from -6 to 6
- adjoint: float32 [5, 125, 32768], P(None, None, 'dom'), may hold values from -6 to 6
- order: int32 [32768], P('dom'), may hold values from 2 to 4
- neighbours: int32 [6, 32768], P(None, 'dom'), may hold values from -1 to 32767, as said below
- owner: int32 [32768, 1], P('dom'), may hold values from 0 to 127; in each aligned block of 256 rows (0 to 255, 256 to 511, ...) at most 4 rows name the same one
- jacobian: float32 [5, 5, 32768], P(None, None, 'dom'), may hold values from -6 to 6
- enrich: float32 [3, 216, 125], replicated, may hold values from -0.5 to 0.5
- volume: float32 [216, 125], replicated, may hold values from -0.5 to 0.5
Outputs:
- indicator: float32 [32768], P('dom')
- moved_state: float32 [5, 125, 65536], P(None, None, 'dom')
- moved_adjoint: float32 [5, 216, 65536], P(None, None, 'dom')
- slot_ids: int32 [65536], P('dom')
- slot_orders: int32 [65536], P('dom')
The draws below stay inside these ranges and needn't reach their ends.
Inputs may be any that keep to these rules, and one draw needn't show every extreme that they name: Faces 0 and 1 join elements along the first mode direction, 2 and 3 along the second, 4 and 5 along the third, with equal orientation of the two other directions; if neighbours[f, e] = g >= 0 then neighbours[f XOR 1, g] = e. Every neighbour across faces 2 to 5 lies on the element's own device; across faces 0 and 1 it lies either on the element's own device or among the last 128 elements of the previous device or the first 128 of the next. Among the elements of one device at most 4 have the same new owner, and some owner gets exactly 4 of them.
All inputs are finite; a program needn't handle non-finite values.
Results may differ from the reference program's by a relative error of at most 0.0003.
Values sent between devices are 32-bit elements; how exact they have to be, the bound alone decides.
No kernel may reach another device: no remote copies, remote signals or barrier semaphores. Data moves between devices by JAX's collectives and lax.ppermute only.
A program may use at most 64 MiB of HBM per device.

```python
import math
import jax
import jax.numpy as jnp
import numpy as np
from jax import lax

FIELDS = 5
MODES = 125
RICH = 216
NR = 8
NA = 16
LAYERS = 2
KE = 256
ELEMENTS = 32768
CAP = 4
N_DOM = 128


def draw_neighbours(key, part):
    key = jax.random.fold_in(key, 11)
    layer_size = NR * NA
    slabs = LAYERS * N_DOM
    key_list = jax.random.split(key, slabs)

    def shuffle(one_key):
        return jax.random.permutation(one_key, layer_size).astype(jnp.int32)
    layout = jax.vmap(shuffle)(key_list)
    slab_index = jnp.broadcast_to(jnp.arange(slabs, dtype=jnp.int32)[:, None], (slabs, layer_size))
    cell_index = jnp.broadcast_to(jnp.arange(layer_size, dtype=jnp.int32)[None, :], (slabs, layer_size))
    radial = cell_index // NA
    beside_all = cell_index % NA

    def index_at(slab_at, radial_at, around_at):
        return slab_at * layer_size + layout[slab_at, radial_at * NA + around_at]
    own_index = index_at(slab_index, radial, beside_all)
    values = []
    below_slab = jnp.clip(slab_index - 1, 0, slabs - 1)
    above_slab = jnp.clip(slab_index + 1, 0, slabs - 1)
    values.append(jnp.where(slab_index > 0, index_at(below_slab, radial, beside_all), -1))
    values.append(jnp.where(slab_index < slabs - 1, index_at(above_slab, radial, beside_all), -1))
    inner = jnp.clip(radial - 1, 0, NR - 1)
    outer_cycle = jnp.clip(radial + 1, 0, NR - 1)
    values.append(jnp.where(radial > 0, index_at(slab_index, inner, beside_all), -1))
    values.append(jnp.where(radial < NR - 1, index_at(slab_index, outer_cycle, beside_all), -1))
    values.append(index_at(slab_index, radial, (beside_all + NA - 1) % NA))
    values.append(index_at(slab_index, radial, (beside_all + 1) % NA))
    stacked = jnp.stack(values).reshape(6, slabs * layer_size).astype(jnp.int32)
    result = jnp.full((6, slabs * layer_size), -1, jnp.int32)
    return result.at[:, own_index.reshape(-1)].set(stacked)


def with_ends(entries, stream_key, least, largest):
    spot = [jax.random.randint(jax.random.fold_in(stream_key, axis), (), 0, length) for axis, length in enumerate(entries.shape)]
    longest = entries.shape.index(max(entries.shape))
    neighbour = spot[:longest] + [(spot[longest] + 1) % entries.shape[longest]] + spot[longest + 1:]
    return entries.at[tuple(spot)].set(least).at[tuple(neighbour)].set(largest)


def block_levels(rng, dims, pieces, smallest, largest):
    def one(axis_at, shards_of):
        steps = jax.random.uniform(jax.random.fold_in(jax.random.fold_in(rng, 6), axis_at), (shards_of,), jnp.float32, smallest / len(pieces), largest / len(pieces))
        return jnp.repeat(jnp.exp(steps), dims[axis_at] // shards_of).reshape((-1,) + (1,) * (len(dims) - axis_at - 1))

    factor_of = one(*pieces[0])
    for cut in pieces[1:]:
        factor_of = factor_of * one(*cut)
    return factor_of


def shared_out(rng, own, number, rows, amount, top, limit, lean):
    order = jax.random.permutation(rng, amount)
    heavy_load, common = load_shares(amount, rows * top, limit, lean, True), load_shares(amount, rows * top, limit, lean, False)
    places = jnp.arange(amount)

    def named(tallies, turn):
        used = int((tallies > 0).sum())
        fixed = max(1, used // 4)
        moved = fixed + (places - fixed + turn * (used - fixed)) % max(1, amount - fixed)
        return jnp.zeros((amount,), jnp.int32).at[order[jnp.where(places < fixed, places, moved)]].set(jnp.asarray(tallies, jnp.int32))

    tallies = jnp.where(number % 4 == 0, named(heavy_load, number // 4), named(common, number - number // 4 - 1))
    mixed = jax.random.permutation(jax.random.fold_in(own, 3), amount)
    donor, sink = mixed[0:amount // 2 * 2:2], mixed[1:amount // 2 * 2:2]
    margin = jnp.minimum(tallies[donor] - 1, limit - tallies[sink]) // 2
    margin = jnp.where((donor == order[0]) | (sink == order[0]) | (tallies[sink] == 0), 0, jnp.maximum(margin, 0))
    moved = jax.random.randint(jax.random.fold_in(own, 4), (amount // 2,), 0, 1 << 20) % (margin + 1)
    tallies = tallies.at[donor].add(-moved).at[sink].add(moved)
    items = jnp.searchsorted(jnp.cumsum(tallies), jnp.arange(rows * top), side="right").astype(jnp.int32)
    table = items.reshape(top, rows).T
    table = table[jax.random.permutation(jax.random.fold_in(own, 1), rows)]
    turn = jax.random.randint(jax.random.fold_in(own, 2), (rows, 1), 0, top)
    return jnp.take_along_axis(table, (jnp.arange(top)[None, :] + turn) % top, axis=1)


def load_shares(count, total, limit, skew, full):
    portions = [(1 << 20) // math.isqrt(standing ** skew) + 1 for standing in range(1, count + 1)]
    largest = limit if full else min(limit, max(-(-total // count), total * portions[0] // sum(portions)))
    least = 1 if total - largest >= count - 1 else 0
    given, spare = [largest] + [least] * (count - 1), total - largest - least * (count - 1)
    while spare > 0:
        movable = [i for i in range(1, count) if given[i] < largest] or [i for i in range(1, count) if given[i] < limit]
        pool, budget = sum([portions[i] for i in movable]), spare
        for i in movable:
            more = min(limit - given[i], max(1, budget * portions[i] // pool), spare)
            given[i] = given[i] + more
            spare = spare - more
    return np.array(given)


def scatter_about(own_key, shape, scale, reach, shards=(), kind=jnp.bfloat16):
    factor_of = block_levels(own_key, shape, shards, -0.22, 0.18) if shards else 1.0
    values = jax.random.normal(own_key, shape, jnp.float32) * scale * factor_of
    return jnp.minimum(jnp.maximum(values, -reach), reach).astype(kind)


def setup_inputs(seed: int = 0) -> dict:
    seeds = jax.random.split(jax.random.key(seed), 9)
    state = scatter_about(seeds[0], (FIELDS, MODES, ELEMENTS), 1.0, 6.0, ((2, 128),), jnp.float32)
    adjoint = scatter_about(seeds[1], (FIELDS, MODES, ELEMENTS), 1.0, 6.0, ((2, 128),), jnp.float32)
    order = with_ends(jax.random.randint(seeds[2], (ELEMENTS,), 2, 5), jax.random.fold_in(seeds[2], 1), 2, 4).astype(jnp.int32)
    neighbours = draw_neighbours(jax.random.fold_in(seeds[8], 71), 0)
    owner_keys = jax.random.split(jax.random.fold_in(seeds[4], 1), ELEMENTS // KE)
    owner_turns = jax.random.permutation(jax.random.fold_in(seeds[4], 3), ELEMENTS // KE)
    owner = jax.vmap(lambda own, number: shared_out(jax.random.fold_in(seeds[4], 2), own, number, KE, N_DOM, 1, CAP, 2))(owner_keys, owner_turns).reshape((ELEMENTS, 1))
    jacobian = scatter_about(seeds[5], (FIELDS, FIELDS, ELEMENTS), 0.45, 6.0, ((2, 128),), jnp.float32)
    enrich = scatter_about(seeds[6], (3, RICH, MODES), MODES ** -0.5, 0.5, (), jnp.float32)
    volume = scatter_about(seeds[7], (RICH, MODES), MODES ** -0.5, 0.5, (), jnp.float32)
    return dict(state=state, adjoint=adjoint, order=order, neighbours=neighbours, owner=owner, jacobian=jacobian, enrich=enrich, volume=volume)


precise = lax.Precision.HIGHEST


def mode_tables():
    small_modes = jnp.arange(125, dtype=jnp.int32)
    small_coords = jnp.stack([small_modes // 25, (small_modes // 5) % 5, small_modes % 5])
    rich_modes = jnp.arange(216, dtype=jnp.int32)
    rich_coords = jnp.stack([rich_modes // 36, (rich_modes // 6) % 6, rich_modes % 6])
    order_levels = jnp.arange(3, dtype=jnp.int32)[:, None] + 2
    keep_in = (jnp.max(small_coords, axis=0)[None, :] <= order_levels).astype(jnp.float32)
    keep_new = (jnp.max(rich_coords, axis=0)[None, :] == order_levels + 1).astype(jnp.float32)
    face_modes = jnp.arange(25, dtype=jnp.int32)
    trace_rows = []
    lift_rows = []
    for face_index in range(6):
        normal_axis = face_index // 2
        tangent_axes = [entry for entry in range(3) if entry != normal_axis]
        normal_index = small_coords[normal_axis]
        tangent_index = small_coords[tangent_axes[0]] * 5 + small_coords[tangent_axes[1]]
        rich_normal = rich_coords[normal_axis]
        rich_tangent = rich_coords[tangent_axes[0]] * 5 + rich_coords[tangent_axes[1]]
        in_range = (rich_coords[tangent_axes[0]] < 5) & (rich_coords[tangent_axes[1]] < 5)
        if face_index % 2 == 0:
            parity = jnp.where(normal_index % 2 == 1, -1.0, 1.0).astype(jnp.float32)
            rich_parity = jnp.where(rich_normal % 2 == 1, -1.0, 1.0).astype(jnp.float32)
        else:
            parity = jnp.ones((125,), jnp.float32)
            rich_parity = jnp.ones((216,), jnp.float32)
        trace_rows.append((face_modes[:, None] == tangent_index[None, :]).astype(jnp.float32) * parity[None, :])
        lift_weight = rich_parity * (2 * rich_normal + 1).astype(jnp.float32) * 0.5
        matches = (rich_tangent[:, None] == face_modes[None, :]) & in_range[:, None]
        lift_rows.append(matches.astype(jnp.float32) * lift_weight[:, None])
    return keep_in, keep_new, jnp.stack(trace_rows), jnp.stack(lift_rows)


def enrich_adjoint(coarse, choose, keep_new, enrich):
    field_count = coarse.shape[0]
    column_count = coarse.shape[2]
    as_cube = coarse.reshape(field_count, 5, 5, 5, column_count)
    embedded = jnp.pad(as_cube, ((0, 0), (0, 1), (0, 1), (0, 1), (0, 0))).reshape(field_count, 216, column_count)
    new_modes = jnp.zeros((field_count, 216, column_count), jnp.float32)
    for degree in range(3):
        partial_term = jnp.einsum("nm,cme->cne", enrich[degree], coarse, precision=precise)
        new_modes = new_modes + partial_term * (keep_new[degree][:, None] * choose[degree][None, :])[None]
    return embedded, new_modes


def residual_of(coarse_state, traces, neighbour_traces, jacobian, volume, lift_table):
    jump_term = neighbour_traces - traces
    face_flux = jnp.zeros_like(jump_term)
    weighted = jnp.zeros_like(coarse_state)
    for field_index in range(jacobian.shape[0]):
        face_flux = face_flux + jacobian[:, field_index][None, :, None, :] * jump_term[:, field_index][:, None, :, :]
        weighted = weighted + jacobian[:, field_index][:, None, :] * coarse_state[field_index][None]
    residual = jnp.einsum("nm,cme->cne", volume, weighted, precision=precise)
    residual = residual + jnp.einsum("fnq,fcqe->cne", lift_table, face_flux, precision=precise)
    return residual


def reference(state, adjoint, order, neighbours, owner, jacobian, enrich, volume):
    field_count = state.shape[0]
    keep_in, keep_new, trace_table, lift_table = mode_tables()
    choose = (order[None, :] - 2 == jnp.arange(3, dtype=jnp.int32)[:, None]).astype(jnp.float32)
    keep_mask = jnp.sum(choose[:, None, :] * keep_in[:, :, None], axis=0)
    coarse_state = state * keep_mask[None]
    coarse_adjoint = adjoint * keep_mask[None]
    embedded, new_modes = enrich_adjoint(coarse_adjoint, choose, keep_new, enrich)
    traces = jnp.einsum("fqm,cme->fcqe", trace_table, coarse_state, precision=precise)
    gathered = []
    for face_index in range(6):
        picked = jnp.take(traces[face_index ^ 1], jnp.clip(neighbours[face_index], 0, ELEMENTS - 1), axis=2)
        gathered.append(picked * (neighbours[face_index] >= 0).astype(jnp.float32)[None, None, :])
    neighbour_traces = jnp.stack(gathered)
    residual = residual_of(coarse_state, traces, neighbour_traces, jacobian, volume, lift_table)
    indicator = jnp.abs(jnp.sum(new_modes * residual, axis=(0, 1))) * (1.0 / 216.0)
    targets = owner[:, 0]
    blocks = targets.reshape(N_DOM, KE)
    owner_hits = (blocks[:, :, None] == jnp.arange(N_DOM, dtype=jnp.int32)[None, None, :]).astype(jnp.int32)
    arrival_rank = jnp.sum((jnp.cumsum(owner_hits, axis=1) - 1) * owner_hits, axis=2).reshape(-1)
    element_index = jnp.arange(ELEMENTS, dtype=jnp.int32)
    column = targets * (N_DOM * CAP) + (element_index // KE) * CAP + arrival_rank
    total = N_DOM * N_DOM * CAP
    moved_state = jnp.zeros((field_count, 125, total), jnp.float32).at[:, :, column].set(coarse_state)
    moved_adjoint = jnp.zeros((field_count, 216, total), jnp.float32).at[:, :, column].set(embedded + new_modes)
    slot_ids = jnp.full((total,), -1, jnp.int32).at[column].set(element_index)
    slot_orders = jnp.zeros((total,), jnp.int32).at[column].set(order)
    return (indicator, moved_state, moved_adjoint, slot_ids, slot_orders)
```

```python
import functools
import jax
import jax.numpy as jnp
import numpy as np
from jax import lax
from jax.experimental import pallas as pl
from jax.experimental.pallas import tpu as pltpu
from jax.sharding import PartitionSpec as P

FIELDS = 5
MODES = 125
RICH = 216
KE = 256
CAP = 4
ND = 128
HALF = 128
QP = 32
VMEM = 48 * 1024 * 1024


def tables():
    m = np.arange(MODES)
    small = np.stack([m // 25, m // 5 % 5, m % 5])
    n = np.arange(RICH)
    rich = np.stack([n // 36, n // 6 % 6, n % 6])
    trace = np.zeros((6 * QP, MODES), np.float32)
    lift = np.zeros((RICH, 6 * QP), np.float32)
    for f in range(6):
        d = f // 2
        t1, t2 = [a for a in range(3) if a != d]
        s = -1.0 if f % 2 == 0 else 1.0
        trace[f * QP + small[t1] * 5 + small[t2], m] = s ** small[d]
        ok = (rich[t1] < 5) & (rich[t2] < 5)
        weight = s ** rich[d] * (2 * rich[d] + 1) * 0.5
        lift[n[ok], (f * QP + rich[t1] * 5 + rich[t2])[ok]] = weight[ok]
    embed = np.zeros((RICH, 128), np.float32)
    embed[small[0] * 36 + small[1] * 6 + small[2], m] = 1.0
    rich_top = rich.max(axis=0).astype(np.float32)[:, None]
    return trace, lift, embed, rich_top


TRACE, LIFT, EMBED, RICH_TOP = tables()


def dot(a, b):
    return lax.dot_general(a, b, (((1,), (0,)), ((), ())), preferred_element_type=jnp.float32)


def dot_nt(a, b):
    return lax.dot_general(a, b, (((1,), (1,)), ((), ())), preferred_element_type=jnp.float32)


def parts(x):
    high = x.astype(jnp.bfloat16)
    return high, (x - high.astype(jnp.float32)).astype(jnp.bfloat16)


def exact_dot(a, x):
    high, low = parts(x)
    return dot(a, high) + dot(a, low)


def dot_exact(x, a):
    high, low = parts(x)
    return dot(high, a) + dot(low, a)


def dot_three(a, x):
    a_high, a_low = a
    high, low = parts(x)
    return dot(a_high, high) + (dot(a_high, low) + dot(a_low, high))


def kept(order_row):
    m = lax.broadcasted_iota(jnp.int32, (MODES, KE), 0)
    i = (m * 41) >> 10
    rest = m - i * 25
    j = (rest * 13) >> 6
    k = rest - j * 5
    return jnp.maximum(jnp.maximum(i, j), k) <= order_row


def pack_kernel(order_ref, owner_ref, state_ref, adjoint_ref, out_ref, sel_ref, x_ref):
    @pl.when(pl.program_id(0) == 0)
    def _():
        hits = owner_ref[...] == lax.broadcasted_iota(jnp.int32, (ND, KE), 0)
        before = lax.broadcasted_iota(jnp.int32, (KE, KE), 0) < lax.broadcasted_iota(
            jnp.int32, (KE, KE), 1
        )
        ones = hits.astype(jnp.float32).astype(jnp.bfloat16)
        count = dot(ones, before.astype(jnp.float32).astype(jnp.bfloat16))
        for r in range(CAP):
            sel = jnp.where(hits & (count == float(r)), 1.0, 0.0)
            sel_ref[r * ND : (r + 1) * ND, :] = sel.astype(jnp.bfloat16)
        local = lax.broadcasted_iota(jnp.int32, (1, KE), 1)
        x_ref[125:126, :] = (local + 1).astype(jnp.float32)
        x_ref[126:127, :] = order_ref[...].astype(jnp.float32)
        x_ref[127:128, :] = jnp.zeros((1, KE), jnp.float32)
        x_ref[253:256, :] = jnp.zeros((3, KE), jnp.float32)

    keep = kept(order_ref[...])
    x_ref[0:MODES, :] = jnp.where(keep, state_ref[0], 0.0)
    x_ref[128 : 128 + MODES, :] = jnp.where(keep, adjoint_ref[0], 0.0)
    high, low = parts(x_ref[...])
    for r in range(CAP):
        sel = sel_ref[r * ND : (r + 1) * ND, :]
        rows = dot_nt(sel, high) + dot_nt(sel, low)
        out_ref[:, r, :] = rows[:, 0:128]
        out_ref[:, CAP + r, :] = rows[:, 128:256]


def pack(order_row, owner_row, state, adjoint):
    row = pl.BlockSpec((1, KE), lambda t: (0, 0))
    field = pl.BlockSpec((1, MODES, KE), lambda t: (t, 0, 0))
    return pl.pallas_call(
        pack_kernel,
        grid=(FIELDS,),
        in_specs=[row, row, field, field],
        out_specs=pl.BlockSpec((ND, 8, 128), lambda t: (0, t, 0)),
        out_shape=jax.ShapeDtypeStruct((ND, 8 * FIELDS, 128), jnp.float32),
        scratch_shapes=[
            pltpu.VMEM((CAP * ND, KE), jnp.bfloat16),
            pltpu.VMEM((256, KE), jnp.float32),
        ],
        compiler_params=pltpu.CompilerParams(vmem_limit_bytes=VMEM),
        name="pack",
    )(order_row, owner_row, state, adjoint)


def edge_kernel(order_ref, state_ref, trace_ref, first_ref, last_ref):
    keep = kept(order_ref[...])
    for c in range(FIELDS):
        coarse = jnp.where(keep, state_ref[c], 0.0)
        rows = exact_dot(trace_ref[0 : 2 * QP, :], coarse)
        for f in range(2):
            first_ref[f, c * QP : (c + 1) * QP, :] = rows[f * QP : (f + 1) * QP, :HALF]
            last_ref[f, c * QP : (c + 1) * QP, :] = rows[f * QP : (f + 1) * QP, KE - HALF :]


def edges(order_row, state, trace):
    shape = jax.ShapeDtypeStruct((2, FIELDS * QP, HALF), jnp.float32)
    return pl.pallas_call(
        edge_kernel,
        out_shape=(shape, shape),
        compiler_params=pltpu.CompilerParams(vmem_limit_bytes=VMEM),
        name="edges",
    )(order_row, state, trace)


def indicator_kernel(
    device_ref,
    order_ref,
    near_ref,
    state_ref,
    adjoint_ref,
    jacobian_ref,
    enrich_ref,
    volume_ref,
    before_ref,
    after_ref,
    trace_ref,
    lift_ref,
    top_ref,
    out_ref,
    rows_ref,
    traces_ref,
    jump_ref,
    flux_ref,
    coarse_ref,
):
    order_row = order_ref[...]
    keep = kept(order_row)
    start = device_ref[0] * KE
    for c in range(FIELDS):
        coarse = jnp.where(keep, state_ref[c], 0.0)
        coarse_ref[c] = coarse
        rows = exact_dot(trace_ref[...], coarse)
        for f in range(6):
            traces_ref[f, c * QP : (c + 1) * QP, :] = rows[f * QP : (f + 1) * QP, :]
    for f in range(6):
        near = near_ref[f : f + 1, :]
        local = jnp.where(near >= 0, near - start, -(1 << 20))

        def picks(count, shift):
            at = lax.broadcasted_iota(jnp.int32, (count, KE), 0)
            return jnp.where(at == local + shift, 1.0, 0.0).astype(jnp.bfloat16)

        other = f ^ 1
        found = dot_exact(traces_ref[other], picks(KE, 0))
        if f < 2:
            found = found + dot_exact(before_ref[other], picks(HALF, HALF))
            found = found + dot_exact(after_ref[other], picks(HALF, -KE))
        jump_ref[f] = found - traces_ref[f]
    top = top_ref[...]
    enrich = jnp.where(
        top == 3.0,
        enrich_ref[0],
        jnp.where(top == 4.0, enrich_ref[1], jnp.where(top == 5.0, enrich_ref[2], 0.0)),
    )
    enrich_parts = parts(enrich)
    rows_ref[0:RICH, 0:MODES] = enrich_parts[0]
    rows_ref[RICH:, 0:MODES] = enrich_parts[1]
    rows_ref[:, MODES:] = jnp.zeros((2 * RICH, 3), jnp.bfloat16)
    volume_parts = parts(volume_ref[...])
    new_mask = top == order_row.astype(jnp.float32) + 1.0
    total = jnp.zeros((RICH, KE), jnp.float32)
    for c in range(FIELDS):
        factors = jacobian_ref[c]
        weighted = factors[0:1, :] * coarse_ref[0]
        for h in range(1, FIELDS):
            weighted = weighted + factors[h : h + 1, :] * coarse_ref[h]
        for f in range(6):
            flux = factors[0:1, :] * jump_ref[f, 0:QP, :]
            for h in range(1, FIELDS):
                flux = flux + factors[h : h + 1, :] * jump_ref[f, h * QP : (h + 1) * QP, :]
            flux_ref[f * QP : (f + 1) * QP, :] = flux
        residual = dot_three(volume_parts, weighted) + exact_dot(lift_ref[...], flux_ref[...])
        new = dot_three(enrich_parts, jnp.where(keep, adjoint_ref[c], 0.0))
        total = total + jnp.where(new_mask, new, 0.0) * residual
    out_ref[...] = jnp.abs(jnp.sum(total, axis=0, keepdims=True)) * (1.0 / 216.0)


def indicators(device, order_row, near, state, adjoint, jacobian, enrich, volume, before, after):
    space = pl.BlockSpec(memory_space=pltpu.VMEM)
    return pl.pallas_call(
        indicator_kernel,
        in_specs=[pl.BlockSpec(memory_space=pltpu.SMEM)] + [space] * 12,
        out_specs=(space, space),
        out_shape=(
            jax.ShapeDtypeStruct((1, KE), jnp.float32),
            jax.ShapeDtypeStruct((2 * RICH, 128), jnp.bfloat16),
        ),
        scratch_shapes=[
            pltpu.VMEM((6, FIELDS * QP, KE), jnp.float32),
            pltpu.VMEM((6, FIELDS * QP, KE), jnp.float32),
            pltpu.VMEM((6 * QP, KE), jnp.float32),
            pltpu.VMEM((FIELDS, MODES, KE), jnp.float32),
        ],
        compiler_params=pltpu.CompilerParams(vmem_limit_bytes=VMEM),
        name="indicators",
    )(
        device,
        order_row,
        near,
        state,
        adjoint,
        jacobian,
        enrich,
        volume,
        before,
        after,
        jnp.asarray(TRACE, jnp.bfloat16),
        jnp.asarray(LIFT, jnp.bfloat16),
        jnp.asarray(RICH_TOP),
    )


def unpack_kernel(in_ref, enrich_ref, embed_ref, eye_ref, top_ref, state_ref, adjoint_ref, ids_ref, orders_ref):
    block = in_ref[...].reshape(ND // 2, 2, 8, 128)
    even, odd = block[:, 0], block[:, 1]
    upper = lax.broadcasted_iota(jnp.int32, even.shape, 1) >= CAP
    slots = ND * CAP
    state = jnp.where(upper, pltpu.roll(odd, CAP, 1), even).reshape(slots, 128)
    adjoint = jnp.where(upper, odd, pltpu.roll(even, CAP, 1)).reshape(slots, 128)
    high, low = parts(state)
    eye = eye_ref[...]
    moved = dot_nt(eye, high) + dot_nt(eye, low)
    state_ref[0] = moved[0:MODES, :]
    order_row = moved[126:127, :]
    high, low = parts(adjoint)
    embed = embed_ref[...]
    old = dot_nt(embed, high) + dot_nt(embed, low)
    top_rows, bottom = enrich_ref[0:RICH, :], enrich_ref[RICH:, :]
    new = dot_nt(top_rows, high) + (dot_nt(top_rows, low) + dot_nt(bottom, high))
    adjoint_ref[0] = old + jnp.where(top_ref[...] == order_row + 1.0, new, 0.0)

    @pl.when(pl.program_id(0) == 0)
    def _():
        id_row = moved[125:126, :].astype(jnp.int32)
        first = (lax.broadcasted_iota(jnp.int32, (1, slots), 1) >> 2) * KE
        ids_ref[...] = jnp.where(id_row > 0, first + id_row - 1, -1)
        orders_ref[...] = order_row.astype(jnp.int32)


def unpack(received, enrich_rows):
    slots = ND * CAP
    whole = lambda a: pl.BlockSpec(a, lambda t: (0,) * len(a))
    return pl.pallas_call(
        unpack_kernel,
        grid=(FIELDS,),
        in_specs=[
            pl.BlockSpec((ND, 8, 128), lambda t: (0, t, 0)),
            whole((2 * RICH, 128)),
            whole((RICH, 128)),
            whole((128, 128)),
            whole((RICH, 1)),
        ],
        out_specs=(
            pl.BlockSpec((1, MODES, slots), lambda t: (t, 0, 0)),
            pl.BlockSpec((1, RICH, slots), lambda t: (t, 0, 0)),
            whole((1, slots)),
            whole((1, slots)),
        ),
        out_shape=(
            jax.ShapeDtypeStruct((FIELDS, MODES, slots), jnp.float32),
            jax.ShapeDtypeStruct((FIELDS, RICH, slots), jnp.float32),
            jax.ShapeDtypeStruct((1, slots), jnp.int32),
            jax.ShapeDtypeStruct((1, slots), jnp.int32),
        ),
        compiler_params=pltpu.CompilerParams(vmem_limit_bytes=VMEM),
        name="unpack",
    )(
        received,
        enrich_rows,
        jnp.asarray(EMBED, jnp.bfloat16),
        jnp.asarray(np.eye(128), jnp.bfloat16),
        jnp.asarray(RICH_TOP),
    )


def body(state, adjoint, order, neighbours, owner, jacobian, enrich, volume):
    device = lax.axis_index("dom")
    order_row = order.reshape(1, KE)
    message = pack(order_row, owner.reshape(1, KE), state, adjoint)
    received = lax.all_to_all(message, "dom", split_axis=0, concat_axis=0, tiled=True)
    first, last = edges(order_row, state, jnp.asarray(TRACE, jnp.bfloat16))
    up = [(i, i + 1) for i in range(ND - 1)]
    down = [(i + 1, i) for i in range(ND - 1)]
    before = lax.ppermute(last, "dom", up)
    after = lax.ppermute(first, "dom", down)
    indicator, enrich_rows = indicators(
        device.reshape(1),
        order_row,
        neighbours,
        state,
        adjoint,
        jacobian,
        enrich,
        volume,
        before,
        after,
    )
    moved_state, moved_adjoint, ids, orders = unpack(received, enrich_rows)
    return (
        indicator.reshape(KE),
        moved_state,
        moved_adjoint,
        ids.reshape(ND * CAP),
        orders.reshape(ND * CAP),
    )


def solution(mesh):
    wide = P(None, None, "dom")
    in_specs = (wide, wide, P("dom"), P(None, "dom"), P("dom", None), wide, P(), P())
    out_specs = (P("dom"), wide, wide, P("dom"), P("dom"))
    return jax.shard_map(body, mesh=mesh, in_specs=in_specs, out_specs=out_specs, check_vma=False)
```

```python
import jax
import jax.numpy as jnp
import numpy as np
from jax import lax
from jax.experimental import pallas as pl
from jax.experimental.pallas import tpu as pltpu
from jax.sharding import PartitionSpec as P

FIELDS = 5
MODES = 125
RICH = 216
KE = 256
CAP = 4
ND = 128
HALF = 128
QP = 32
VMEM = 48 * 1024 * 1024


def tables():
    m = np.arange(MODES)
    small = np.stack([m // 25, m // 5 % 5, m % 5])
    n = np.arange(RICH)
    rich = np.stack([n // 36, n // 6 % 6, n % 6])
    trace = np.zeros((6 * QP, MODES), np.float32)
    lift = np.zeros((RICH, 6 * QP), np.float32)
    for f in range(6):
        d = f // 2
        t1, t2 = [a for a in range(3) if a != d]
        s = -1.0 if f % 2 == 0 else 1.0
        trace[f * QP + small[t1] * 5 + small[t2], m] = s ** small[d]
        ok = (rich[t1] < 5) & (rich[t2] < 5)
        weight = s ** rich[d] * (2 * rich[d] + 1) * 0.5
        lift[n[ok], (f * QP + rich[t1] * 5 + rich[t2])[ok]] = weight[ok]
    rich_top = rich.max(axis=0).astype(np.float32)[:, None]
    return trace, lift, rich_top


TRACE, LIFT, RICH_TOP = tables()


def hbm(x):
    return pltpu.with_memory_space_constraint(x, pltpu.HBM)


def dot(a, b):
    return lax.dot_general(a, b, (((1,), (0,)), ((), ())), preferred_element_type=jnp.float32)


def dot_nt(a, b):
    return lax.dot_general(a, b, (((1,), (1,)), ((), ())), preferred_element_type=jnp.float32)


def parts(x):
    high = x.astype(jnp.bfloat16)
    return high, (x - high.astype(jnp.float32)).astype(jnp.bfloat16)


def exact_dot(a, x):
    high, low = parts(x)
    return dot(a, high) + dot(a, low)


def dot_exact(x, a):
    high, low = parts(x)
    return dot(high, a) + dot(low, a)


def dot_three(a, x):
    a_high, a_low = a
    high, low = parts(x)
    return dot(a_high, high) + (dot(a_high, low) + dot(a_low, high))


def kept(order_row):
    m = lax.broadcasted_iota(jnp.int32, (MODES, KE), 0)
    i = (m * 41) >> 10
    rest = m - i * 25
    j = (rest * 13) >> 6
    k = rest - j * 5
    return jnp.maximum(jnp.maximum(i, j), k) <= order_row


def pack_kernel(
    order_hbm,
    owner_hbm,
    state_hbm,
    adjoint_hbm,
    out_hbm,
    order_ref,
    owner_ref,
    state_ref,
    adjoint_ref,
    x_ref,
    out_ref,
    in_sems,
    out_sems,
):
    small = [
        pltpu.make_async_copy(order_hbm, order_ref, in_sems.at[0]),
        pltpu.make_async_copy(owner_hbm, owner_ref, in_sems.at[1]),
    ]
    fields = [
        (
            pltpu.make_async_copy(state_hbm.at[t], state_ref.at[t], in_sems.at[2 + 2 * t]),
            pltpu.make_async_copy(adjoint_hbm.at[t], adjoint_ref.at[t], in_sems.at[3 + 2 * t]),
        )
        for t in range(FIELDS)
    ]
    for copy in small:
        copy.start()
    for pair in fields:
        for copy in pair:
            copy.start()
    before = lax.broadcasted_iota(jnp.int32, (KE, KE), 0) < lax.broadcasted_iota(
        jnp.int32, (KE, KE), 1
    )
    before = jnp.where(before, 1.0, 0.0).astype(jnp.bfloat16)
    local = lax.broadcasted_iota(jnp.int32, (1, KE), 1)
    x_ref[125:126, :] = (local + 1).astype(jnp.float32)
    x_ref[127:128, :] = jnp.zeros((1, KE), jnp.float32)
    x_ref[253:256, :] = jnp.zeros((3, KE), jnp.float32)
    for copy in small:
        copy.wait()
    order_row = order_ref[...]
    x_ref[126:127, :] = order_row.astype(jnp.float32)
    hits = owner_ref[...] == lax.broadcasted_iota(jnp.int32, (ND, KE), 0)
    count = dot(jnp.where(hits, 1.0, 0.0).astype(jnp.bfloat16), before)
    sel = jnp.concatenate(
        [
            jnp.where(hits & (count == float(r)), 1.0, 0.0).astype(jnp.bfloat16)
            for r in range(CAP)
        ],
        axis=0,
    )
    keep = kept(order_row)
    sends = []
    for t in range(FIELDS):
        for copy in fields[t]:
            copy.wait()
        x_ref[0:MODES, :] = jnp.where(keep, state_ref[t], 0.0)
        x_ref[128 : 128 + MODES, :] = jnp.where(keep, adjoint_ref[t], 0.0)
        high, low = parts(x_ref[...])
        rows = dot_nt(sel, high) + dot_nt(sel, low)
        for r in range(CAP):
            out_ref[t, :, r, :] = rows[r * ND : (r + 1) * ND, 0:128]
            out_ref[t, :, CAP + r, :] = rows[r * ND : (r + 1) * ND, 128:256]
        send = pltpu.make_async_copy(
            out_ref.at[t], out_hbm.at[:, pl.ds(8 * t, 8), :], out_sems.at[t]
        )
        send.start()
        sends.append(send)
    for send in sends:
        send.wait()


def pack(order_row, owner_row, state, adjoint):
    far = pl.BlockSpec(memory_space=pltpu.HBM)
    return pl.pallas_call(
        pack_kernel,
        in_specs=[far] * 4,
        out_specs=far,
        out_shape=pltpu.HBM((ND, 8 * FIELDS, 128), jnp.float32),
        scratch_shapes=[
            pltpu.VMEM((1, KE), jnp.int32),
            pltpu.VMEM((1, KE), jnp.int32),
            pltpu.VMEM((FIELDS, MODES, KE), jnp.float32),
            pltpu.VMEM((FIELDS, MODES, KE), jnp.float32),
            pltpu.VMEM((256, KE), jnp.float32),
            pltpu.VMEM((FIELDS, ND, 8, 128), jnp.float32),
            pltpu.SemaphoreType.DMA((2 + 2 * FIELDS,)),
            pltpu.SemaphoreType.DMA((FIELDS,)),
        ],
        compiler_params=pltpu.CompilerParams(vmem_limit_bytes=VMEM),
        name="pack",
    )(hbm(order_row), hbm(owner_row), hbm(state), hbm(adjoint))


def edge_kernel(order_ref, state_ref, trace_ref, first_ref, last_ref):
    keep = kept(order_ref[...])
    for c in range(FIELDS):
        coarse = jnp.where(keep, state_ref[c], 0.0)
        rows = exact_dot(trace_ref[0 : 2 * QP, :], coarse)
        for f in range(2):
            first_ref[f, c * QP : (c + 1) * QP, :] = rows[f * QP : (f + 1) * QP, :HALF]
            last_ref[f, c * QP : (c + 1) * QP, :] = rows[f * QP : (f + 1) * QP, KE - HALF :]


def edges(order_row, state, trace):
    shape = jax.ShapeDtypeStruct((2, FIELDS * QP, HALF), jnp.float32)
    return pl.pallas_call(
        edge_kernel,
        out_shape=(shape, shape),
        compiler_params=pltpu.CompilerParams(vmem_limit_bytes=VMEM),
        name="edges",
    )(order_row, state, trace)


def indicator_kernel(
    device_ref,
    order_ref,
    near_ref,
    state_ref,
    adjoint_ref,
    jacobian_ref,
    enrich_ref,
    volume_ref,
    trace_ref,
    lift_ref,
    lift_edge_ref,
    top_ref,
    own_ref,
    rows_ref,
    edge_ref,
    picks_ref,
    traces_ref,
    jump_ref,
    flux_ref,
    coarse_ref,
):
    order_row = order_ref[...]
    keep = kept(order_row)
    start = device_ref[0] * KE
    for c in range(FIELDS):
        coarse = jnp.where(keep, state_ref[c], 0.0)
        coarse_ref[c] = coarse
        rows = exact_dot(trace_ref[...], coarse)
        for f in range(6):
            traces_ref[f, c * QP : (c + 1) * QP, :] = rows[f * QP : (f + 1) * QP, :]
    for f in range(6):
        near = near_ref[f : f + 1, :]
        local = jnp.where(near >= 0, near - start, -(1 << 20))
        at = lax.broadcasted_iota(jnp.int32, (KE, KE), 0)
        own = jnp.where(at == local, 1.0, 0.0).astype(jnp.bfloat16)
        jump_ref[f] = dot_exact(traces_ref[f ^ 1], own) - traces_ref[f]
        if f < 2:
            place = jnp.where(at < HALF, at - HALF, at + HALF)
            picks_ref[f] = jnp.where(place == local, 1.0, 0.0).astype(jnp.bfloat16)
    top = top_ref[...]
    enrich = jnp.where(
        top == 3.0,
        enrich_ref[0],
        jnp.where(top == 4.0, enrich_ref[1], jnp.where(top == 5.0, enrich_ref[2], 0.0)),
    )
    enrich_parts = parts(enrich)
    rows_ref[...] = jnp.zeros(rows_ref.shape, jnp.bfloat16)
    rows_ref[0:RICH, 0:MODES] = enrich_parts[0]
    rows_ref[0:RICH, 128 : 128 + MODES] = enrich_parts[0]
    rows_ref[RICH:, 0:MODES] = enrich_parts[1]
    volume_parts = parts(volume_ref[...])
    new_mask = top == order_row.astype(jnp.float32) + 1.0
    total = jnp.zeros((RICH, KE), jnp.float32)
    for c in range(FIELDS):
        factors = jacobian_ref[c]
        weighted = factors[0:1, :] * coarse_ref[0]
        for h in range(1, FIELDS):
            weighted = weighted + factors[h : h + 1, :] * coarse_ref[h]
        for f in range(6):
            flux = factors[0:1, :] * jump_ref[f, 0:QP, :]
            for h in range(1, FIELDS):
                flux = flux + factors[h : h + 1, :] * jump_ref[f, h * QP : (h + 1) * QP, :]
            flux_ref[f * QP : (f + 1) * QP, :] = flux
        residual = dot_three(volume_parts, weighted) + exact_dot(lift_ref[...], flux_ref[...])
        new = dot_three(enrich_parts, jnp.where(keep, adjoint_ref[c], 0.0))
        new = jnp.where(new_mask, new, 0.0)
        total = total + new * residual
        lifted = exact_dot(lift_edge_ref[...], new)
        for f in range(2):
            for h in range(FIELDS):
                term = factors[h : h + 1, :] * lifted[f * QP : (f + 1) * QP, :]
                rows = slice(h * QP, (h + 1) * QP)
                edge_ref[f, rows, :] = term if c == 0 else edge_ref[f, rows, :] + term
    own_ref[...] = jnp.sum(total, axis=0, keepdims=True)


def own_indicators(device, order_row, near, state, adjoint, jacobian, enrich, volume):
    space = pl.BlockSpec(memory_space=pltpu.VMEM)
    return pl.pallas_call(
        indicator_kernel,
        in_specs=[pl.BlockSpec(memory_space=pltpu.SMEM)] + [space] * 11,
        out_specs=(space,) * 4,
        out_shape=(
            pltpu.HBM((1, KE), jnp.float32),
            pltpu.HBM((2 * RICH, 256), jnp.bfloat16),
            pltpu.HBM((2, FIELDS * QP, KE), jnp.float32),
            pltpu.HBM((2, KE, KE), jnp.bfloat16),
        ),
        scratch_shapes=[
            pltpu.VMEM((6, FIELDS * QP, KE), jnp.float32),
            pltpu.VMEM((6, FIELDS * QP, KE), jnp.float32),
            pltpu.VMEM((6 * QP, KE), jnp.float32),
            pltpu.VMEM((FIELDS, MODES, KE), jnp.float32),
        ],
        compiler_params=pltpu.CompilerParams(vmem_limit_bytes=VMEM),
        name="own_indicators",
    )(
        device,
        order_row,
        near,
        state,
        adjoint,
        jacobian,
        enrich,
        volume,
        jnp.asarray(TRACE, jnp.bfloat16),
        jnp.asarray(LIFT, jnp.bfloat16),
        jnp.asarray(LIFT[:, : 2 * QP].T, jnp.bfloat16),
        jnp.asarray(RICH_TOP),
    )


def unpack_kernel(
    in_ref,
    rows_hbm,
    own_hbm,
    edge_hbm,
    picks_hbm,
    before_hbm,
    after_hbm,
    state_hbm,
    adjoint_hbm,
    ids_hbm,
    orders_hbm,
    indicator_hbm,
    rows_ref,
    own_ref,
    edge_ref,
    picks_ref,
    halo_ref,
    state_ref,
    adjoint_ref,
    ids_ref,
    orders_ref,
    indicator_ref,
    in_sems,
    out_sems,
):
    loads = [
        pltpu.make_async_copy(rows_hbm, rows_ref, in_sems.at[0]),
        pltpu.make_async_copy(own_hbm, own_ref, in_sems.at[1]),
        pltpu.make_async_copy(edge_hbm, edge_ref, in_sems.at[2]),
        pltpu.make_async_copy(picks_hbm, picks_ref, in_sems.at[3]),
        pltpu.make_async_copy(before_hbm, halo_ref.at[0], in_sems.at[4]),
        pltpu.make_async_copy(after_hbm, halo_ref.at[1], in_sems.at[5]),
    ]
    for copy in loads:
        copy.start()
    slots = ND * CAP
    n = lax.broadcasted_iota(jnp.int32, (RICH, 256), 0)
    i = (n * 57) >> 11
    rest = n - i * 36
    j = (rest * 43) >> 8
    k = rest - j * 6
    top = jnp.maximum(jnp.maximum(i, j), k)
    m = lax.broadcasted_iota(jnp.int32, (RICH, 256), 1) & 127
    embed = jnp.where((top < 5) & (m == i * 25 + j * 5 + k), 1.0, 0.0).astype(jnp.bfloat16)
    m = lax.broadcasted_iota(jnp.int32, (128, 256), 1) & 127
    eye = jnp.where(m == lax.broadcasted_iota(jnp.int32, (128, 256), 0), 1.0, 0.0)
    eye = eye.astype(jnp.bfloat16)
    top = jnp.concatenate([top, top], axis=1)
    upper = lax.broadcasted_iota(jnp.int32, (ND // 2, 8, 128), 1) >= CAP
    stores = []

    def store(source, target):
        copy = pltpu.make_async_copy(source, target, out_sems.at[len(stores)])
        copy.start()
        stores.append(copy)

    def doubled(x):
        high, low = parts(x.reshape(slots, 128))
        return jnp.concatenate([high, low], axis=1)

    for t in range(FIELDS):
        block = in_ref[:, 8 * t : 8 * t + 8, :].reshape(ND // 2, 2, 8, 128)
        even, odd = block[:, 0], block[:, 1]
        moved = dot_nt(eye, doubled(jnp.where(upper, pltpu.roll(odd, CAP, 1), even)))
        state_ref[t] = moved[0:MODES, :]
        store(state_ref.at[t], state_hbm.at[t])
        if t == 0:
            id_row = moved[125:126, :].astype(jnp.int32)
            order_row = moved[126:127, :].astype(jnp.int32)
            new_mask = top == order_row + 1
            first = (lax.broadcasted_iota(jnp.int32, (1, slots), 1) >> 2) * KE
            ids_ref[...] = jnp.where(id_row > 0, first + id_row - 1, -1)
            orders_ref[...] = order_row
            loads[0].wait()
        adjoint = doubled(jnp.where(upper, odd, pltpu.roll(even, CAP, 1)))
        new = dot_nt(rows_ref[0:RICH, :], adjoint) + dot_nt(
            rows_ref[RICH:, 0:128], adjoint[:, 0:128]
        )
        adjoint_ref[t] = dot_nt(embed, adjoint) + jnp.where(new_mask, new, 0.0)
        store(adjoint_ref.at[t], adjoint_hbm.at[t])
        if t == 0:
            store(ids_ref, ids_hbm)
            store(orders_ref, orders_hbm)
    for copy in loads[1:]:
        copy.wait()
    total = own_ref[...]
    for f in range(2):
        halo = jnp.concatenate([halo_ref[0, f ^ 1], halo_ref[1, f ^ 1]], axis=1)
        found = dot_exact(halo, picks_ref[f])
        total = total + jnp.sum(found * edge_ref[f], axis=0, keepdims=True)
    indicator_ref[...] = jnp.abs(total) * (1.0 / 216.0)
    store(indicator_ref, indicator_hbm)
    for copy in stores:
        copy.wait()


def unpack(received, rows, own, edge, picks, before, after):
    slots = ND * CAP
    far = pl.BlockSpec(memory_space=pltpu.HBM)
    shapes = (
        ((FIELDS, MODES, slots), jnp.float32),
        ((FIELDS, RICH, slots), jnp.float32),
        ((1, slots), jnp.int32),
        ((1, slots), jnp.int32),
        ((1, KE), jnp.float32),
    )
    return pl.pallas_call(
        unpack_kernel,
        in_specs=[pl.BlockSpec(memory_space=pltpu.VMEM)] + [far] * 6,
        out_specs=(far,) * 5,
        out_shape=tuple(pltpu.HBM(*a) for a in shapes),
        scratch_shapes=[
            pltpu.VMEM((2 * RICH, 256), jnp.bfloat16),
            pltpu.VMEM((1, KE), jnp.float32),
            pltpu.VMEM((2, FIELDS * QP, KE), jnp.float32),
            pltpu.VMEM((2, KE, KE), jnp.bfloat16),
            pltpu.VMEM((2, 2, FIELDS * QP, HALF), jnp.float32),
        ]
        + [pltpu.VMEM(*a) for a in shapes]
        + [pltpu.SemaphoreType.DMA((6,)), pltpu.SemaphoreType.DMA((2 * FIELDS + 3,))],
        compiler_params=pltpu.CompilerParams(vmem_limit_bytes=VMEM),
        name="unpack",
    )(received, hbm(rows), hbm(own), hbm(edge), hbm(picks), hbm(before), hbm(after))


def body(state, adjoint, order, neighbours, owner, jacobian, enrich, volume):
    device = lax.axis_index("dom")
    order_row = order.reshape(1, KE)
    message = pack(order_row, owner.reshape(1, KE), state, adjoint)
    received = lax.all_to_all(message, "dom", split_axis=0, concat_axis=0, tiled=True)
    first, last = edges(order_row, state, jnp.asarray(TRACE, jnp.bfloat16))
    up = [(i, i + 1) for i in range(ND - 1)]
    down = [(i + 1, i) for i in range(ND - 1)]
    before = lax.ppermute(last, "dom", up)
    after = lax.ppermute(first, "dom", down)
    own, rows, edge, picks = own_indicators(
        device.reshape(1), order_row, neighbours, state, adjoint, jacobian, enrich, volume
    )
    moved_state, moved_adjoint, ids, orders, indicator = unpack(
        received, rows, own, edge, picks, before, after
    )
    return (
        indicator.reshape(KE),
        moved_state,
        moved_adjoint,
        ids.reshape(ND * CAP),
        orders.reshape(ND * CAP),
    )


def solution(mesh):
    wide = P(None, None, "dom")
    in_specs = (wide, wide, P("dom"), P(None, "dom"), P("dom", None), wide, P(), P())
    out_specs = (P("dom"), wide, wide, P("dom"), P("dom"))
    return jax.shard_map(body, mesh=mesh, in_specs=in_specs, out_specs=out_specs, check_vma=False)
```

```python
import jax
import jax.numpy as jnp
import numpy as np
from jax import lax
from jax.experimental import pallas as pl
from jax.experimental.pallas import tpu as pltpu
from jax.sharding import PartitionSpec as P

FIELDS = 5
MODES = 125
RICH = 216
KE = 256
CAP = 4
ND = 128
HALF = 128
QP = 32
VMEM = 48 * 1024 * 1024


def tables():
    m = np.arange(MODES)
    small = np.stack([m // 25, m // 5 % 5, m % 5])
    n = np.arange(RICH)
    rich = np.stack([n // 36, n // 6 % 6, n % 6])
    trace = np.zeros((6 * QP, MODES), np.float32)
    lift = np.zeros((RICH, 6 * QP), np.float32)
    for f in range(6):
        d = f // 2
        t1, t2 = [a for a in range(3) if a != d]
        s = -1.0 if f % 2 == 0 else 1.0
        trace[f * QP + small[t1] * 5 + small[t2], m] = s ** small[d]
        ok = (rich[t1] < 5) & (rich[t2] < 5)
        weight = s ** rich[d] * (2 * rich[d] + 1) * 0.5
        lift[n[ok], (f * QP + rich[t1] * 5 + rich[t2])[ok]] = weight[ok]
    rich_top = rich.max(axis=0).astype(np.float32)[:, None]
    return trace, lift, rich_top


TRACE, LIFT, RICH_TOP = tables()


def hbm(x):
    return pltpu.with_memory_space_constraint(x, pltpu.HBM)


def dot(a, b):
    return lax.dot_general(a, b, (((1,), (0,)), ((), ())), preferred_element_type=jnp.float32)


def dot_nt(a, b):
    return lax.dot_general(a, b, (((1,), (1,)), ((), ())), preferred_element_type=jnp.float32)


def parts(x):
    high = x.astype(jnp.bfloat16)
    return high, (x - high.astype(jnp.float32)).astype(jnp.bfloat16)


def exact_dot(a, x):
    high, low = parts(x)
    return dot(a, high) + dot(a, low)


def dot_exact(x, a):
    high, low = parts(x)
    return dot(high, a) + dot(low, a)


def dot_three(a, x):
    a_high, a_low = a
    high, low = parts(x)
    return dot(a_high, high) + (dot(a_high, low) + dot(a_low, high))


def kept(order_row):
    m = lax.broadcasted_iota(jnp.int32, (MODES, KE), 0)
    i = (m * 41) >> 10
    rest = m - i * 25
    j = (rest * 13) >> 6
    k = rest - j * 5
    return jnp.maximum(jnp.maximum(i, j), k) <= order_row


def pack_kernel(
    order_hbm,
    owner_hbm,
    state_hbm,
    adjoint_hbm,
    out_hbm,
    order_ref,
    owner_ref,
    state_ref,
    adjoint_ref,
    x_ref,
    out_ref,
    in_sems,
    out_sems,
):
    small = [
        pltpu.make_async_copy(order_hbm, order_ref, in_sems.at[0]),
        pltpu.make_async_copy(owner_hbm, owner_ref, in_sems.at[1]),
    ]
    fields = [
        pltpu.make_async_copy(state_hbm, state_ref, in_sems.at[2]),
        pltpu.make_async_copy(adjoint_hbm, adjoint_ref, in_sems.at[3]),
    ]
    for copy in small:
        copy.start()
    for copy in fields:
        copy.start()
    before = lax.broadcasted_iota(jnp.int32, (KE, KE), 0) < lax.broadcasted_iota(
        jnp.int32, (KE, KE), 1
    )
    before = jnp.where(before, 1.0, 0.0).astype(jnp.bfloat16)
    local = lax.broadcasted_iota(jnp.int32, (1, KE), 1)
    for t in range(FIELDS):
        x_ref[t, 125:126, :] = (local + 1).astype(jnp.float32)
        x_ref[t, 127:128, :] = jnp.zeros((1, KE), jnp.float32)
        x_ref[t, 253:256, :] = jnp.zeros((3, KE), jnp.float32)
    for copy in small:
        copy.wait()
    order_row = order_ref[...]
    for t in range(FIELDS):
        x_ref[t, 126:127, :] = order_row.astype(jnp.float32)
    hits = owner_ref[...] == lax.broadcasted_iota(jnp.int32, (ND, KE), 0)
    count = dot(jnp.where(hits, 1.0, 0.0).astype(jnp.bfloat16), before)
    rank = jnp.sum(jnp.where(hits, count, 0.0), axis=0, keepdims=True).astype(jnp.int32)
    slot = owner_ref[...] * CAP + rank
    sel = jnp.where(slot == lax.broadcasted_iota(jnp.int32, (CAP * ND, KE), 0), 1.0, 0.0)
    sel = sel.astype(jnp.bfloat16)
    upper = lax.broadcasted_iota(jnp.int32, (ND // 2, 8, 128), 1) >= CAP
    keep = kept(order_row)
    sends = []

    def prepare(t):
        x_ref[t, 0:MODES, :] = jnp.where(keep, state_ref[t], 0.0)
        x_ref[t, 128 : 128 + MODES, :] = jnp.where(keep, adjoint_ref[t], 0.0)
        return parts(x_ref[t])

    def gather(pair):
        return dot_nt(sel, pair[0]) + dot_nt(sel, pair[1])

    def send(t, rows):
        low_rows = rows[:, 0:128].reshape(ND // 2, 8, 128)
        high_rows = rows[:, 128:256].reshape(ND // 2, 8, 128)
        out_ref[t, :, 0] = jnp.where(upper, pltpu.roll(high_rows, CAP, 1), low_rows)
        out_ref[t, :, 1] = jnp.where(upper, high_rows, pltpu.roll(low_rows, CAP, 1))
        copy = pltpu.make_async_copy(
            out_ref.at[t], out_hbm.at[:, :, pl.ds(8 * t, 8), :], out_sems.at[t]
        )
        copy.start()
        sends.append(copy)

    for copy in fields:
        copy.wait()
    for t in range(FIELDS):
        send(t, gather(prepare(t)))
    for copy in sends:
        copy.wait()


def pack(order_row, owner_row, state, adjoint):
    far = pl.BlockSpec(memory_space=pltpu.HBM)
    return pl.pallas_call(
        pack_kernel,
        in_specs=[far] * 4,
        out_specs=far,
        out_shape=pltpu.HBM((ND // 2, 2, 8 * FIELDS, 128), jnp.float32),
        scratch_shapes=[
            pltpu.VMEM((1, KE), jnp.int32),
            pltpu.VMEM((1, KE), jnp.int32),
            pltpu.VMEM((FIELDS, MODES, KE), jnp.float32),
            pltpu.VMEM((FIELDS, MODES, KE), jnp.float32),
            pltpu.VMEM((FIELDS, 256, KE), jnp.float32),
            pltpu.VMEM((FIELDS, ND // 2, 2, 8, 128), jnp.float32),
            pltpu.SemaphoreType.DMA((4,)),
            pltpu.SemaphoreType.DMA((FIELDS,)),
        ],
        compiler_params=pltpu.CompilerParams(vmem_limit_bytes=VMEM),
        name="pack",
    )(hbm(order_row), hbm(owner_row), hbm(state), hbm(adjoint)).reshape(ND, 8 * FIELDS, 128)


def edge_kernel(order_ref, state_ref, trace_ref, first_ref, last_ref):
    keep = kept(order_ref[...])
    for c in range(FIELDS):
        coarse = jnp.where(keep, state_ref[c], 0.0)
        rows = exact_dot(trace_ref[0 : 2 * QP, :], coarse)
        for f in range(2):
            first_ref[f, c * QP : (c + 1) * QP, :] = rows[f * QP : (f + 1) * QP, :HALF]
            last_ref[f, c * QP : (c + 1) * QP, :] = rows[f * QP : (f + 1) * QP, KE - HALF :]


def edges(order_row, state, trace):
    shape = jax.ShapeDtypeStruct((2, FIELDS * QP, HALF), jnp.float32)
    return pl.pallas_call(
        edge_kernel,
        out_shape=(shape, shape),
        compiler_params=pltpu.CompilerParams(vmem_limit_bytes=VMEM),
        name="edges",
    )(order_row, state, trace)


def indicator_kernel(
    device_ref,
    order_ref,
    near_ref,
    state_ref,
    adjoint_ref,
    jacobian_ref,
    enrich_ref,
    volume_ref,
    trace_ref,
    lift_ref,
    lift_edge_ref,
    top_ref,
    own_ref,
    rows_ref,
    edge_ref,
    picks_ref,
    traces_ref,
    jump_ref,
    flux_ref,
    coarse_ref,
):
    order_row = order_ref[...]
    keep = kept(order_row)
    start = device_ref[0] * KE
    for c in range(FIELDS):
        coarse = jnp.where(keep, state_ref[c], 0.0)
        coarse_ref[c] = coarse
        rows = exact_dot(trace_ref[...], coarse)
        for f in range(6):
            traces_ref[f, c * QP : (c + 1) * QP, :] = rows[f * QP : (f + 1) * QP, :]
    for f in range(6):
        near = near_ref[f : f + 1, :]
        local = jnp.where(near >= 0, near - start, -(1 << 20))
        at = lax.broadcasted_iota(jnp.int32, (KE, KE), 0)
        own = jnp.where(at == local, 1.0, 0.0).astype(jnp.bfloat16)
        jump_ref[f] = dot_exact(traces_ref[f ^ 1], own) - traces_ref[f]
        if f < 2:
            place = jnp.where(at < HALF, at - HALF, at + HALF)
            picks_ref[f] = jnp.where(place == local, 1.0, 0.0).astype(jnp.bfloat16)
    top = top_ref[...]
    enrich = jnp.where(
        top == 3.0,
        enrich_ref[0],
        jnp.where(top == 4.0, enrich_ref[1], jnp.where(top == 5.0, enrich_ref[2], 0.0)),
    )
    enrich_parts = parts(enrich)
    rows_ref[...] = jnp.zeros(rows_ref.shape, jnp.bfloat16)
    rows_ref[0:RICH, 0:MODES] = enrich_parts[0]
    rows_ref[0:RICH, 128 : 128 + MODES] = enrich_parts[0]
    rows_ref[RICH:, 0:MODES] = enrich_parts[1]
    volume_parts = parts(volume_ref[...])
    new_mask = top == order_row.astype(jnp.float32) + 1.0
    total = jnp.zeros((RICH, KE), jnp.float32)
    for c in range(FIELDS):
        factors = jacobian_ref[c]
        weighted = factors[0:1, :] * coarse_ref[0]
        for h in range(1, FIELDS):
            weighted = weighted + factors[h : h + 1, :] * coarse_ref[h]
        for f in range(6):
            flux = factors[0:1, :] * jump_ref[f, 0:QP, :]
            for h in range(1, FIELDS):
                flux = flux + factors[h : h + 1, :] * jump_ref[f, h * QP : (h + 1) * QP, :]
            flux_ref[f * QP : (f + 1) * QP, :] = flux
        residual = dot_three(volume_parts, weighted) + exact_dot(lift_ref[...], flux_ref[...])
        new = dot_three(enrich_parts, jnp.where(keep, adjoint_ref[c], 0.0))
        new = jnp.where(new_mask, new, 0.0)
        total = total + new * residual
        lifted = exact_dot(lift_edge_ref[...], new)
        for f in range(2):
            for h in range(FIELDS):
                term = factors[h : h + 1, :] * lifted[f * QP : (f + 1) * QP, :]
                rows = slice(h * QP, (h + 1) * QP)
                edge_ref[f, rows, :] = term if c == 0 else edge_ref[f, rows, :] + term
    own_ref[...] = jnp.sum(total, axis=0, keepdims=True)


def own_indicators(device, order_row, near, state, adjoint, jacobian, enrich, volume):
    space = pl.BlockSpec(memory_space=pltpu.VMEM)
    return pl.pallas_call(
        indicator_kernel,
        in_specs=[pl.BlockSpec(memory_space=pltpu.SMEM)] + [space] * 11,
        out_specs=(space,) * 4,
        out_shape=(
            pltpu.HBM((1, KE), jnp.float32),
            pltpu.HBM((2 * RICH, 256), jnp.bfloat16),
            pltpu.HBM((2, FIELDS * QP, KE), jnp.float32),
            pltpu.HBM((2, KE, KE), jnp.bfloat16),
        ),
        scratch_shapes=[
            pltpu.VMEM((6, FIELDS * QP, KE), jnp.float32),
            pltpu.VMEM((6, FIELDS * QP, KE), jnp.float32),
            pltpu.VMEM((6 * QP, KE), jnp.float32),
            pltpu.VMEM((FIELDS, MODES, KE), jnp.float32),
        ],
        compiler_params=pltpu.CompilerParams(vmem_limit_bytes=VMEM),
        name="own_indicators",
    )(
        device,
        order_row,
        near,
        state,
        adjoint,
        jacobian,
        enrich,
        volume,
        jnp.asarray(TRACE, jnp.bfloat16),
        jnp.asarray(LIFT, jnp.bfloat16),
        jnp.asarray(LIFT[:, : 2 * QP].T, jnp.bfloat16),
        jnp.asarray(RICH_TOP),
    )


def unpack_kernel(
    in_ref,
    rows_hbm,
    own_hbm,
    edge_hbm,
    picks_hbm,
    before_hbm,
    after_hbm,
    state_hbm,
    adjoint_hbm,
    ids_hbm,
    orders_hbm,
    indicator_hbm,
    rows_ref,
    own_ref,
    edge_ref,
    picks_ref,
    halo_ref,
    state_ref,
    adjoint_ref,
    ids_ref,
    orders_ref,
    indicator_ref,
    in_sems,
    out_sems,
):
    loads = [
        pltpu.make_async_copy(rows_hbm, rows_ref.at[pl.ds(0, 2 * RICH)], in_sems.at[0]),
        pltpu.make_async_copy(own_hbm, own_ref, in_sems.at[1]),
        pltpu.make_async_copy(edge_hbm, edge_ref, in_sems.at[2]),
        pltpu.make_async_copy(picks_hbm, picks_ref, in_sems.at[3]),
        pltpu.make_async_copy(before_hbm, halo_ref.at[0], in_sems.at[4]),
        pltpu.make_async_copy(after_hbm, halo_ref.at[1], in_sems.at[5]),
    ]
    for copy in loads:
        copy.start()
    slots = ND * CAP
    n = lax.broadcasted_iota(jnp.int32, (RICH, 256), 0)
    i = (n * 57) >> 11
    rest = n - i * 36
    j = (rest * 43) >> 8
    k = rest - j * 6
    top = jnp.maximum(jnp.maximum(i, j), k)
    m = lax.broadcasted_iota(jnp.int32, (RICH, 256), 1) & 127
    embed = jnp.where((top < 5) & (m == i * 25 + j * 5 + k), 1.0, 0.0).astype(jnp.bfloat16)
    rows_ref[2 * RICH :, :] = embed
    m = lax.broadcasted_iota(jnp.int32, (128, 256), 1) & 127
    eye = jnp.where(m == lax.broadcasted_iota(jnp.int32, (128, 256), 0), 1.0, 0.0)
    eye = eye.astype(jnp.bfloat16)
    top = jnp.concatenate([top, top], axis=1)
    upper = lax.broadcasted_iota(jnp.int32, (ND // 2, 8, 128), 1) >= CAP
    stores = []

    def store(source, target):
        copy = pltpu.make_async_copy(source, target, out_sems.at[len(stores)])
        copy.start()
        stores.append(copy)

    def doubled(x):
        high, low = parts(x.reshape(slots, 128))
        return jnp.concatenate([high, low], axis=1)

    def finish():
        for copy in loads[1:]:
            copy.wait()
        total = own_ref[...]
        for f in range(2):
            halo = jnp.concatenate([halo_ref[0, f ^ 1], halo_ref[1, f ^ 1]], axis=1)
            found = dot_exact(halo, picks_ref[f])
            total = total + jnp.sum(found * edge_ref[f], axis=0, keepdims=True)
        indicator_ref[...] = jnp.abs(total) * (1.0 / 216.0)

    def split(t):
        block = in_ref[:, 8 * t : 8 * t + 8, :].reshape(ND // 2, 2, 8, 128)
        even, odd = block[:, 0], block[:, 1]
        state = jnp.where(upper, pltpu.roll(odd, CAP, 1), even)
        return state, jnp.where(upper, odd, pltpu.roll(even, CAP, 1))

    def put_state(t, state):
        moved = state.reshape(slots, 128).T
        state_ref[t] = moved[0:MODES, :]
        return moved

    def put_adjoint(t, both, new_mask):
        new = both[0:RICH] + both[RICH : 2 * RICH]
        adjoint_ref[t] = both[2 * RICH :] + jnp.where(new_mask, new, 0.0)

    def labels(moved):
        id_row = moved[125:126, :].astype(jnp.int32)
        order_row = moved[126:127, :].astype(jnp.int32)
        first = (lax.broadcasted_iota(jnp.int32, (1, slots), 1) >> 2) * KE
        ids_ref[...] = jnp.where(id_row > 0, first + id_row - 1, -1)
        orders_ref[...] = order_row
        return top == order_row + 1

    moves = []
    for t in range(FIELDS):
        state, adjoint = split(t)
        moved = put_state(t, state)
        if t == 0:
            new_mask = labels(moved)
    store(state_ref, state_hbm)
    loads[0].wait()
    for t in range(FIELDS):
        put_adjoint(t, dot_nt(rows_ref[...], doubled(split(t)[1])), new_mask)
        if t == 2:
            finish()
            store(indicator_ref, indicator_hbm)
            store(ids_ref, ids_hbm)
            store(orders_ref, orders_hbm)
        store(adjoint_ref.at[t], adjoint_hbm.at[t])
    for copy in stores:
        copy.wait()


def unpack(received, rows, own, edge, picks, before, after):
    slots = ND * CAP
    far = pl.BlockSpec(memory_space=pltpu.HBM)
    shapes = (
        ((FIELDS, MODES, slots), jnp.float32),
        ((FIELDS, RICH, slots), jnp.float32),
        ((1, slots), jnp.int32),
        ((1, slots), jnp.int32),
        ((1, KE), jnp.float32),
    )
    return pl.pallas_call(
        unpack_kernel,
        in_specs=[pl.BlockSpec(memory_space=pltpu.VMEM)] + [far] * 6,
        out_specs=(far,) * 5,
        out_shape=tuple(pltpu.HBM(*a) for a in shapes),
        scratch_shapes=[
            pltpu.VMEM((3 * RICH, 256), jnp.bfloat16),
            pltpu.VMEM((1, KE), jnp.float32),
            pltpu.VMEM((2, FIELDS * QP, KE), jnp.float32),
            pltpu.VMEM((2, KE, KE), jnp.bfloat16),
            pltpu.VMEM((2, 2, FIELDS * QP, HALF), jnp.float32),
        ]
        + [pltpu.VMEM(*a) for a in shapes]
        + [pltpu.SemaphoreType.DMA((6,)), pltpu.SemaphoreType.DMA((2 * FIELDS + 3,))],
        compiler_params=pltpu.CompilerParams(vmem_limit_bytes=VMEM),
        name="unpack",
    )(received, hbm(rows), hbm(own), hbm(edge), hbm(picks), hbm(before), hbm(after))


def body(state, adjoint, order, neighbours, owner, jacobian, enrich, volume):
    device = lax.axis_index("dom")
    order_row = order.reshape(1, KE)
    message = pack(order_row, owner.reshape(1, KE), state, adjoint)
    received = lax.all_to_all(message, "dom", split_axis=0, concat_axis=0, tiled=True)
    first, last = edges(order_row, state, jnp.asarray(TRACE, jnp.bfloat16))
    up = [(i, i + 1) for i in range(ND - 1)]
    down = [(i + 1, i) for i in range(ND - 1)]
    before = lax.ppermute(last, "dom", up)
    after = lax.ppermute(first, "dom", down)
    own, rows, edge, picks = own_indicators(
        device.reshape(1), order_row, neighbours, state, adjoint, jacobian, enrich, volume
    )
    moved_state, moved_adjoint, ids, orders, indicator = unpack(
        received, rows, own, edge, picks, before, after
    )
    return (
        indicator.reshape(KE),
        moved_state,
        moved_adjoint,
        ids.reshape(ND * CAP),
        orders.reshape(ND * CAP),
    )


def solution(mesh):
    wide = P(None, None, "dom")
    in_specs = (wide, wide, P("dom"), P(None, "dom"), P("dom", None), wide, P(), P())
    out_specs = (P("dom"), wide, wide, P("dom"), P("dom"))
    return jax.shard_map(body, mesh=mesh, in_specs=in_specs, out_specs=out_specs, check_vma=False)
```

```python
import jax
import jax.numpy as jnp
import numpy as np
from jax import lax
from jax.experimental import pallas as pl
from jax.experimental.pallas import tpu as pltpu
from jax.sharding import PartitionSpec as P

FIELDS = 5
MODES = 125
RICH = 216
KE = 256
CAP = 4
ND = 128
HALF = 128
QP = 32
LOADS = ((0, 2), (2, 3))
VMEM = 48 * 1024 * 1024


def tables():
    m = np.arange(MODES)
    small = np.stack([m // 25, m // 5 % 5, m % 5])
    n = np.arange(RICH)
    rich = np.stack([n // 36, n // 6 % 6, n % 6])
    trace = np.zeros((6 * QP, MODES), np.float32)
    lift = np.zeros((RICH, 6 * QP), np.float32)
    for f in range(6):
        d = f // 2
        t1, t2 = [a for a in range(3) if a != d]
        s = -1.0 if f % 2 == 0 else 1.0
        trace[f * QP + small[t1] * 5 + small[t2], m] = s ** small[d]
        ok = (rich[t1] < 5) & (rich[t2] < 5)
        weight = s ** rich[d] * (2 * rich[d] + 1) * 0.5
        lift[n[ok], (f * QP + rich[t1] * 5 + rich[t2])[ok]] = weight[ok]
    rich_top = rich.max(axis=0).astype(np.float32)[:, None]
    return trace, lift, rich_top


TRACE, LIFT, RICH_TOP = tables()


def hbm(x):
    return pltpu.with_memory_space_constraint(x, pltpu.HBM)


def dot(a, b):
    return lax.dot_general(a, b, (((1,), (0,)), ((), ())), preferred_element_type=jnp.float32)


def dot_nt(a, b):
    return lax.dot_general(a, b, (((1,), (1,)), ((), ())), preferred_element_type=jnp.float32)


def parts(x):
    high = x.astype(jnp.bfloat16)
    return high, (x - high.astype(jnp.float32)).astype(jnp.bfloat16)


def exact_dot(a, x):
    high, low = parts(x)
    return dot(a, high) + dot(a, low)


def dot_exact(x, a):
    high, low = parts(x)
    return dot(high, a) + dot(low, a)


def dot_three(a, x):
    a_high, a_low = a
    high, low = parts(x)
    return dot(a_high, high) + (dot(a_high, low) + dot(a_low, high))


def kept(order_row):
    m = lax.broadcasted_iota(jnp.int32, (MODES, KE), 0)
    i = (m * 41) >> 10
    rest = m - i * 25
    j = (rest * 13) >> 6
    k = rest - j * 5
    return jnp.maximum(jnp.maximum(i, j), k) <= order_row


def pack_kernel(
    order_hbm,
    owner_hbm,
    state_hbm,
    adjoint_hbm,
    out_hbm,
    order_ref,
    owner_ref,
    state_ref,
    adjoint_ref,
    x_ref,
    out_ref,
    in_sems,
    out_sems,
):
    small = [
        pltpu.make_async_copy(order_hbm, order_ref, in_sems.at[0]),
        pltpu.make_async_copy(owner_hbm, owner_ref, in_sems.at[1]),
    ]
    fields = []
    for first, count in LOADS:
        part = pl.ds(first, count)
        k = len(fields) + 2
        fields.append(pltpu.make_async_copy(state_hbm.at[part], state_ref.at[part], in_sems.at[k]))
        fields.append(
            pltpu.make_async_copy(adjoint_hbm.at[part], adjoint_ref.at[part], in_sems.at[k + 1])
        )
    for copy in small:
        copy.start()
    for copy in fields:
        copy.start()
    before = lax.broadcasted_iota(jnp.int32, (KE, KE), 0) < lax.broadcasted_iota(
        jnp.int32, (KE, KE), 1
    )
    before = jnp.where(before, 1.0, 0.0).astype(jnp.bfloat16)
    local = lax.broadcasted_iota(jnp.int32, (1, KE), 1)
    for t in range(FIELDS):
        x_ref[t, 125:126, :] = (local + 1).astype(jnp.float32)
        x_ref[t, 127:128, :] = jnp.zeros((1, KE), jnp.float32)
        x_ref[t, 253:256, :] = jnp.zeros((3, KE), jnp.float32)
    for copy in small:
        copy.wait()
    order_row = order_ref[...]
    for t in range(FIELDS):
        x_ref[t, 126:127, :] = order_row.astype(jnp.float32)
    hits = owner_ref[...] == lax.broadcasted_iota(jnp.int32, (ND, KE), 0)
    count = dot(jnp.where(hits, 1.0, 0.0).astype(jnp.bfloat16), before)
    rank = jnp.sum(jnp.where(hits, count, 0.0), axis=0, keepdims=True).astype(jnp.int32)
    slot = owner_ref[...] * CAP + rank
    sel = jnp.where(slot == lax.broadcasted_iota(jnp.int32, (CAP * ND, KE), 0), 1.0, 0.0)
    sel = sel.astype(jnp.bfloat16)
    upper = lax.broadcasted_iota(jnp.int32, (ND // 2, 8, 128), 1) >= CAP
    keep = kept(order_row)
    sends = []

    def prepare(t):
        x_ref[t, 0:MODES, :] = jnp.where(keep, state_ref[t], 0.0)
        x_ref[t, 128 : 128 + MODES, :] = jnp.where(keep, adjoint_ref[t], 0.0)
        return parts(x_ref[t])

    def gather(pair):
        return dot_nt(sel, pair[0]) + dot_nt(sel, pair[1])

    def send(t, rows):
        low_rows = rows[:, 0:128].reshape(ND // 2, 8, 128)
        high_rows = rows[:, 128:256].reshape(ND // 2, 8, 128)
        out_ref[t, :, 0] = jnp.where(upper, pltpu.roll(high_rows, CAP, 1), low_rows)
        out_ref[t, :, 1] = jnp.where(upper, high_rows, pltpu.roll(low_rows, CAP, 1))
        copy = pltpu.make_async_copy(
            out_ref.at[t], out_hbm.at[:, :, pl.ds(8 * t, 8), :], out_sems.at[t]
        )
        copy.start()
        sends.append(copy)

    for g, (first, count) in enumerate(LOADS):
        fields[2 * g].wait()
        fields[2 * g + 1].wait()
        for t in range(first, first + count):
            send(t, gather(prepare(t)))
    for copy in sends:
        copy.wait()


def pack(order_row, owner_row, state, adjoint):
    far = pl.BlockSpec(memory_space=pltpu.HBM)
    return pl.pallas_call(
        pack_kernel,
        in_specs=[far] * 4,
        out_specs=far,
        out_shape=pltpu.HBM((ND // 2, 2, 8 * FIELDS, 128), jnp.float32),
        scratch_shapes=[
            pltpu.VMEM((1, KE), jnp.int32),
            pltpu.VMEM((1, KE), jnp.int32),
            pltpu.VMEM((FIELDS, MODES, KE), jnp.float32),
            pltpu.VMEM((FIELDS, MODES, KE), jnp.float32),
            pltpu.VMEM((FIELDS, 256, KE), jnp.float32),
            pltpu.VMEM((FIELDS, ND // 2, 2, 8, 128), jnp.float32),
            pltpu.SemaphoreType.DMA((2 + 2 * len(LOADS),)),
            pltpu.SemaphoreType.DMA((FIELDS,)),
        ],
        compiler_params=pltpu.CompilerParams(vmem_limit_bytes=VMEM),
        name="pack",
    )(hbm(order_row), hbm(owner_row), hbm(state), hbm(adjoint)).reshape(ND, 8 * FIELDS, 128)


def edge_kernel(order_ref, state_ref, trace_ref, first_ref, last_ref):
    keep = kept(order_ref[...])
    for c in range(FIELDS):
        coarse = jnp.where(keep, state_ref[c], 0.0)
        rows = exact_dot(trace_ref[0 : 2 * QP, :], coarse)
        for f in range(2):
            first_ref[f, c * QP : (c + 1) * QP, :] = rows[f * QP : (f + 1) * QP, :HALF]
            last_ref[f, c * QP : (c + 1) * QP, :] = rows[f * QP : (f + 1) * QP, KE - HALF :]


def edges(order_row, state, trace):
    shape = jax.ShapeDtypeStruct((2, FIELDS * QP, HALF), jnp.float32)
    return pl.pallas_call(
        edge_kernel,
        out_shape=(shape, shape),
        compiler_params=pltpu.CompilerParams(vmem_limit_bytes=VMEM),
        name="edges",
    )(order_row, state, trace)


def indicator_kernel(
    device_ref,
    order_ref,
    near_ref,
    state_ref,
    adjoint_ref,
    jacobian_ref,
    enrich_ref,
    volume_ref,
    trace_ref,
    lift_ref,
    lift_edge_ref,
    top_ref,
    own_ref,
    rows_ref,
    edge_ref,
    picks_ref,
    traces_ref,
    jump_ref,
    flux_ref,
    coarse_ref,
):
    order_row = order_ref[...]
    keep = kept(order_row)
    start = device_ref[0] * KE
    for c in range(FIELDS):
        coarse = jnp.where(keep, state_ref[c], 0.0)
        coarse_ref[c] = coarse
        rows = exact_dot(trace_ref[...], coarse)
        for f in range(6):
            traces_ref[f, c * QP : (c + 1) * QP, :] = rows[f * QP : (f + 1) * QP, :]
    for f in range(6):
        near = near_ref[f : f + 1, :]
        local = jnp.where(near >= 0, near - start, -(1 << 20))
        at = lax.broadcasted_iota(jnp.int32, (KE, KE), 0)
        own = jnp.where(at == local, 1.0, 0.0).astype(jnp.bfloat16)
        jump_ref[f] = dot_exact(traces_ref[f ^ 1], own) - traces_ref[f]
        if f < 2:
            place = jnp.where(at < HALF, at - HALF, at + HALF)
            picks_ref[f] = jnp.where(place == local, 1.0, 0.0).astype(jnp.bfloat16)
    top = top_ref[...]
    enrich = jnp.where(
        top == 3.0,
        enrich_ref[0],
        jnp.where(top == 4.0, enrich_ref[1], jnp.where(top == 5.0, enrich_ref[2], 0.0)),
    )
    enrich_parts = parts(enrich)
    rows_ref[...] = jnp.zeros(rows_ref.shape, jnp.bfloat16)
    rows_ref[0:RICH, 0:MODES] = enrich_parts[0]
    rows_ref[0:RICH, 128 : 128 + MODES] = enrich_parts[0]
    rows_ref[RICH:, 0:MODES] = enrich_parts[1]
    volume_parts = parts(volume_ref[...])
    new_mask = top == order_row.astype(jnp.float32) + 1.0
    total = jnp.zeros((RICH, KE), jnp.float32)
    for c in range(FIELDS):
        factors = jacobian_ref[c]
        weighted = factors[0:1, :] * coarse_ref[0]
        for h in range(1, FIELDS):
            weighted = weighted + factors[h : h + 1, :] * coarse_ref[h]
        for f in range(6):
            flux = factors[0:1, :] * jump_ref[f, 0:QP, :]
            for h in range(1, FIELDS):
                flux = flux + factors[h : h + 1, :] * jump_ref[f, h * QP : (h + 1) * QP, :]
            flux_ref[f * QP : (f + 1) * QP, :] = flux
        residual = dot_three(volume_parts, weighted) + exact_dot(lift_ref[...], flux_ref[...])
        new = dot_three(enrich_parts, jnp.where(keep, adjoint_ref[c], 0.0))
        new = jnp.where(new_mask, new, 0.0)
        total = total + new * residual
        lifted = exact_dot(lift_edge_ref[...], new)
        for f in range(2):
            for h in range(FIELDS):
                term = factors[h : h + 1, :] * lifted[f * QP : (f + 1) * QP, :]
                rows = slice(h * QP, (h + 1) * QP)
                edge_ref[f, rows, :] = term if c == 0 else edge_ref[f, rows, :] + term
    own_ref[...] = jnp.sum(total, axis=0, keepdims=True)


def own_indicators(device, order_row, near, state, adjoint, jacobian, enrich, volume):
    space = pl.BlockSpec(memory_space=pltpu.VMEM)
    return pl.pallas_call(
        indicator_kernel,
        in_specs=[pl.BlockSpec(memory_space=pltpu.SMEM)] + [space] * 11,
        out_specs=(space,) * 4,
        out_shape=(
            pltpu.HBM((1, KE), jnp.float32),
            pltpu.HBM((2 * RICH, 256), jnp.bfloat16),
            pltpu.HBM((2, FIELDS * QP, KE), jnp.float32),
            pltpu.HBM((2, KE, KE), jnp.bfloat16),
        ),
        scratch_shapes=[
            pltpu.VMEM((6, FIELDS * QP, KE), jnp.float32),
            pltpu.VMEM((6, FIELDS * QP, KE), jnp.float32),
            pltpu.VMEM((6 * QP, KE), jnp.float32),
            pltpu.VMEM((FIELDS, MODES, KE), jnp.float32),
        ],
        compiler_params=pltpu.CompilerParams(vmem_limit_bytes=VMEM),
        name="own_indicators",
    )(
        device,
        order_row,
        near,
        state,
        adjoint,
        jacobian,
        enrich,
        volume,
        jnp.asarray(TRACE, jnp.bfloat16),
        jnp.asarray(LIFT, jnp.bfloat16),
        jnp.asarray(LIFT[:, : 2 * QP].T, jnp.bfloat16),
        jnp.asarray(RICH_TOP),
    )


def unpack_kernel(
    in_ref,
    rows_hbm,
    own_hbm,
    edge_hbm,
    picks_hbm,
    before_hbm,
    after_hbm,
    state_hbm,
    adjoint_hbm,
    ids_hbm,
    orders_hbm,
    indicator_hbm,
    rows_ref,
    own_ref,
    edge_ref,
    picks_ref,
    halo_ref,
    state_ref,
    adjoint_ref,
    ids_ref,
    orders_ref,
    indicator_ref,
    old_ref,
    in_sems,
    out_sems,
):
    loads = [
        pltpu.make_async_copy(rows_hbm, rows_ref, in_sems.at[0]),
        pltpu.make_async_copy(own_hbm, own_ref, in_sems.at[1]),
        pltpu.make_async_copy(edge_hbm, edge_ref, in_sems.at[2]),
        pltpu.make_async_copy(picks_hbm, picks_ref, in_sems.at[3]),
        pltpu.make_async_copy(before_hbm, halo_ref.at[0], in_sems.at[4]),
        pltpu.make_async_copy(after_hbm, halo_ref.at[1], in_sems.at[5]),
    ]
    for copy in loads:
        copy.start()
    slots = ND * CAP
    n = lax.broadcasted_iota(jnp.int32, (RICH, 128), 0)
    i = (n * 57) >> 11
    rest = n - i * 36
    j = (rest * 43) >> 8
    top = jnp.maximum(jnp.maximum(i, j), rest - j * 6)
    top = jnp.concatenate([top] * CAP, axis=1)
    upper = lax.broadcasted_iota(jnp.int32, (ND // 2, 8, 128), 1) >= CAP
    old_ref[...] = jnp.zeros(old_ref.shape, jnp.float32)
    stores = []

    def store(source, target):
        copy = pltpu.make_async_copy(source, target, out_sems.at[len(stores)])
        copy.start()
        stores.append(copy)

    def finish():
        for copy in loads[1:]:
            copy.wait()
        total = own_ref[...]
        for f in range(2):
            halo = jnp.concatenate([halo_ref[0, f ^ 1], halo_ref[1, f ^ 1]], axis=1)
            found = dot_exact(halo, picks_ref[f])
            total = total + jnp.sum(found * edge_ref[f], axis=0, keepdims=True)
        indicator_ref[...] = jnp.abs(total) * (1.0 / 216.0)

    def split(t):
        block = in_ref[:, 8 * t : 8 * t + 8, :].reshape(ND // 2, 2, 8, 128)
        even, odd = block[:, 0], block[:, 1]
        state = jnp.where(upper, pltpu.roll(odd, CAP, 1), even)
        return state, jnp.where(upper, odd, pltpu.roll(even, CAP, 1))

    def put_state(t, state):
        moved = state.reshape(slots, 128).T
        state_ref[t] = moved[0:MODES, :]
        return moved

    def labels(moved):
        id_row = moved[125:126, :].astype(jnp.int32)
        order_row = moved[126:127, :].astype(jnp.int32)
        first = (lax.broadcasted_iota(jnp.int32, (1, slots), 1) >> 2) * KE
        ids_ref[...] = jnp.where(id_row > 0, first + id_row - 1, -1)
        orders_ref[...] = order_row
        return top == order_row + 1

    for t in range(FIELDS):
        moved = put_state(t, split(t)[0])
        if t == 0:
            new_mask = labels(moved)
    store(state_ref, state_hbm)
    loads[0].wait()
    for t in range(FIELDS):
        turned = split(t)[1].reshape(slots, 128).T
        for g in range(25):
            to = 36 * (g // 5) + 6 * (g % 5)
            old_ref[t % 2, to : to + 5, :] = turned[5 * g : 5 * g + 5, :]
        both = dot(rows_ref[...], jnp.concatenate(parts(turned), axis=0))
        adjoint_ref[t] = jnp.where(new_mask, both[0:RICH] + both[RICH:], old_ref[t % 2])
        if t == 2:
            finish()
            store(indicator_ref, indicator_hbm)
            store(ids_ref, ids_hbm)
            store(orders_ref, orders_hbm)
        store(adjoint_ref.at[t], adjoint_hbm.at[t])
    for copy in stores:
        copy.wait()


def unpack(received, rows, own, edge, picks, before, after):
    slots = ND * CAP
    far = pl.BlockSpec(memory_space=pltpu.HBM)
    shapes = (
        ((FIELDS, MODES, slots), jnp.float32),
        ((FIELDS, RICH, slots), jnp.float32),
        ((1, slots), jnp.int32),
        ((1, slots), jnp.int32),
        ((1, KE), jnp.float32),
    )
    return pl.pallas_call(
        unpack_kernel,
        in_specs=[pl.BlockSpec(memory_space=pltpu.VMEM)] + [far] * 6,
        out_specs=(far,) * 5,
        out_shape=tuple(pltpu.HBM(*a) for a in shapes),
        scratch_shapes=[
            pltpu.VMEM((2 * RICH, 256), jnp.bfloat16),
            pltpu.VMEM((1, KE), jnp.float32),
            pltpu.VMEM((2, FIELDS * QP, KE), jnp.float32),
            pltpu.VMEM((2, KE, KE), jnp.bfloat16),
            pltpu.VMEM((2, 2, FIELDS * QP, HALF), jnp.float32),
        ]
        + [pltpu.VMEM(*a) for a in shapes]
        + [pltpu.VMEM((2, RICH, slots), jnp.float32)]
        + [pltpu.SemaphoreType.DMA((6,)), pltpu.SemaphoreType.DMA((2 * FIELDS + 3,))],
        compiler_params=pltpu.CompilerParams(vmem_limit_bytes=VMEM),
        name="unpack",
    )(received, hbm(rows), hbm(own), hbm(edge), hbm(picks), hbm(before), hbm(after))


def body(state, adjoint, order, neighbours, owner, jacobian, enrich, volume):
    device = lax.axis_index("dom")
    order_row = order.reshape(1, KE)
    message = pack(order_row, owner.reshape(1, KE), state, adjoint)
    received = lax.all_to_all(message, "dom", split_axis=0, concat_axis=0, tiled=True)
    first, last = edges(order_row, state, jnp.asarray(TRACE, jnp.bfloat16))
    up = [(i, i + 1) for i in range(ND - 1)]
    down = [(i + 1, i) for i in range(ND - 1)]
    before = lax.ppermute(last, "dom", up)
    after = lax.ppermute(first, "dom", down)
    own, rows, edge, picks = own_indicators(
        device.reshape(1), order_row, neighbours, state, adjoint, jacobian, enrich, volume
    )
    moved_state, moved_adjoint, ids, orders, indicator = unpack(
        received, rows, own, edge, picks, before, after
    )
    return (
        indicator.reshape(KE),
        moved_state,
        moved_adjoint,
        ids.reshape(ND * CAP),
        orders.reshape(ND * CAP),
    )


def solution(mesh):
    wide = P(None, None, "dom")
    in_specs = (wide, wide, P("dom"), P(None, "dom"), P("dom", None), wide, P(), P())
    out_specs = (P("dom"), wide, wide, P("dom"), P("dom"))
    return jax.shard_map(body, mesh=mesh, in_specs=in_specs, out_specs=out_specs, check_vma=False)
```

```python
import jax
import jax.numpy as jnp
import numpy as np
from jax import lax
from jax.experimental import pallas as pl
from jax.experimental.pallas import tpu as pltpu
from jax.sharding import PartitionSpec as P

FIELDS = 5
MODES = 125
RICH = 216
KE = 256
CAP = 4
ND = 128
HALF = 128
QP = 32
LOADS = ((0, 2), (2, 3))
VMEM = 48 * 1024 * 1024


def tables():
    m = np.arange(MODES)
    small = np.stack([m // 25, m // 5 % 5, m % 5])
    n = np.arange(RICH)
    rich = np.stack([n // 36, n // 6 % 6, n % 6])
    trace = np.zeros((6 * QP, MODES), np.float32)
    lift = np.zeros((RICH, 6 * QP), np.float32)
    for f in range(6):
        d = f // 2
        t1, t2 = [a for a in range(3) if a != d]
        s = -1.0 if f % 2 == 0 else 1.0
        trace[f * QP + small[t1] * 5 + small[t2], m] = s ** small[d]
        ok = (rich[t1] < 5) & (rich[t2] < 5)
        weight = s ** rich[d] * (2 * rich[d] + 1) * 0.5
        lift[n[ok], (f * QP + rich[t1] * 5 + rich[t2])[ok]] = weight[ok]
    rich_top = rich.max(axis=0).astype(np.float32)[:, None]
    return trace, lift, rich_top


TRACE, LIFT, RICH_TOP = tables()


def hbm(x):
    return pltpu.with_memory_space_constraint(x, pltpu.HBM)


def dot(a, b):
    return lax.dot_general(a, b, (((1,), (0,)), ((), ())), preferred_element_type=jnp.float32)


def dot_nt(a, b):
    return lax.dot_general(a, b, (((1,), (1,)), ((), ())), preferred_element_type=jnp.float32)


def parts(x):
    high = x.astype(jnp.bfloat16)
    return high, (x - high.astype(jnp.float32)).astype(jnp.bfloat16)


def exact_dot(a, x):
    high, low = parts(x)
    return dot(a, high) + dot(a, low)


def dot_exact(x, a):
    high, low = parts(x)
    return dot(high, a) + dot(low, a)


def dot_three(a, x):
    a_high, a_low = a
    high, low = parts(x)
    return dot(a_high, high) + (dot(a_high, low) + dot(a_low, high))


def kept(order_row):
    m = lax.broadcasted_iota(jnp.int32, (MODES, KE), 0)
    i = (m * 41) >> 10
    rest = m - i * 25
    j = (rest * 13) >> 6
    k = rest - j * 5
    return jnp.maximum(jnp.maximum(i, j), k) <= order_row


def pack_kernel(
    order_hbm,
    owner_hbm,
    state_hbm,
    adjoint_hbm,
    out_hbm,
    order_ref,
    owner_ref,
    state_ref,
    adjoint_ref,
    x_ref,
    out_ref,
    in_sems,
    out_sems,
):
    small = [
        pltpu.make_async_copy(order_hbm, order_ref, in_sems.at[0]),
        pltpu.make_async_copy(owner_hbm, owner_ref, in_sems.at[1]),
    ]
    fields = []
    for first, count in LOADS:
        part = pl.ds(first, count)
        k = len(fields) + 2
        fields.append(pltpu.make_async_copy(state_hbm.at[part], state_ref.at[part], in_sems.at[k]))
        fields.append(
            pltpu.make_async_copy(adjoint_hbm.at[part], adjoint_ref.at[part], in_sems.at[k + 1])
        )
    for copy in small:
        copy.start()
    for copy in fields:
        copy.start()
    before = lax.broadcasted_iota(jnp.int32, (KE, KE), 0) < lax.broadcasted_iota(
        jnp.int32, (KE, KE), 1
    )
    before = jnp.where(before, 1.0, 0.0).astype(jnp.bfloat16)
    local = lax.broadcasted_iota(jnp.int32, (1, KE), 1)
    for t in range(FIELDS):
        x_ref[t, 125:126, :] = (local + 1).astype(jnp.float32)
        x_ref[t, 127:128, :] = jnp.zeros((1, KE), jnp.float32)
        x_ref[t, 253:256, :] = jnp.zeros((3, KE), jnp.float32)
    for copy in small:
        copy.wait()
    order_row = order_ref[...]
    for t in range(FIELDS):
        x_ref[t, 126:127, :] = order_row.astype(jnp.float32)
    hits = owner_ref[...] == lax.broadcasted_iota(jnp.int32, (ND, KE), 0)
    count = dot(jnp.where(hits, 1.0, 0.0).astype(jnp.bfloat16), before)
    rank = jnp.sum(jnp.where(hits, count, 0.0), axis=0, keepdims=True).astype(jnp.int32)
    slot = owner_ref[...] * CAP + rank
    sel = jnp.where(slot == lax.broadcasted_iota(jnp.int32, (CAP * ND, KE), 0), 1.0, 0.0)
    sel = sel.astype(jnp.bfloat16)
    upper = lax.broadcasted_iota(jnp.int32, (ND // 2, 8, 128), 1) >= CAP
    keep = kept(order_row)
    sends = []

    def prepare(t):
        x_ref[t, 0:MODES, :] = jnp.where(keep, state_ref[t], 0.0)
        x_ref[t, 128 : 128 + MODES, :] = jnp.where(keep, adjoint_ref[t], 0.0)
        return parts(x_ref[t])

    def gather(pair):
        return dot_nt(sel, pair[0]) + dot_nt(sel, pair[1])

    def send(t, rows):
        low_rows = rows[:, 0:128].reshape(ND // 2, 8, 128)
        high_rows = rows[:, 128:256].reshape(ND // 2, 8, 128)
        out_ref[t, :, 0] = jnp.where(upper, pltpu.roll(high_rows, CAP, 1), low_rows)
        out_ref[t, :, 1] = jnp.where(upper, high_rows, pltpu.roll(low_rows, CAP, 1))
        copy = pltpu.make_async_copy(
            out_ref.at[t], out_hbm.at[:, :, pl.ds(8 * t, 8), :], out_sems.at[t]
        )
        copy.start()
        sends.append(copy)

    for g, (first, count) in enumerate(LOADS):
        fields[2 * g].wait()
        fields[2 * g + 1].wait()
        for t in range(first, first + count):
            send(t, gather(prepare(t)))
    for copy in sends:
        copy.wait()


def pack(order_row, owner_row, state, adjoint):
    far = pl.BlockSpec(memory_space=pltpu.HBM)
    return pl.pallas_call(
        pack_kernel,
        in_specs=[far] * 4,
        out_specs=far,
        out_shape=pltpu.HBM((ND // 2, 2, 8 * FIELDS, 128), jnp.float32),
        scratch_shapes=[
            pltpu.VMEM((1, KE), jnp.int32),
            pltpu.VMEM((1, KE), jnp.int32),
            pltpu.VMEM((FIELDS, MODES, KE), jnp.float32),
            pltpu.VMEM((FIELDS, MODES, KE), jnp.float32),
            pltpu.VMEM((FIELDS, 256, KE), jnp.float32),
            pltpu.VMEM((FIELDS, ND // 2, 2, 8, 128), jnp.float32),
            pltpu.SemaphoreType.DMA((2 + 2 * len(LOADS),)),
            pltpu.SemaphoreType.DMA((FIELDS,)),
        ],
        compiler_params=pltpu.CompilerParams(vmem_limit_bytes=VMEM),
        name="pack",
    )(hbm(order_row), hbm(owner_row), hbm(state), hbm(adjoint)).reshape(ND, 8 * FIELDS, 128)


def edge_kernel(order_ref, state_ref, trace_ref, first_ref, last_ref):
    keep = kept(order_ref[...])
    for c in range(FIELDS):
        coarse = jnp.where(keep, state_ref[c], 0.0)
        rows = exact_dot(trace_ref[0 : 2 * QP, :], coarse)
        for f in range(2):
            first_ref[f, c * QP : (c + 1) * QP, :] = rows[f * QP : (f + 1) * QP, :HALF]
            last_ref[f, c * QP : (c + 1) * QP, :] = rows[f * QP : (f + 1) * QP, KE - HALF :]


def edges(order_row, state, trace):
    shape = jax.ShapeDtypeStruct((2, FIELDS * QP, HALF), jnp.float32)
    return pl.pallas_call(
        edge_kernel,
        out_shape=(shape, shape),
        compiler_params=pltpu.CompilerParams(vmem_limit_bytes=VMEM),
        name="edges",
    )(order_row, state, trace)


def indicator_kernel(
    device_ref,
    order_ref,
    near_ref,
    state_ref,
    adjoint_ref,
    jacobian_ref,
    enrich_ref,
    volume_ref,
    trace_ref,
    lift_ref,
    lift_edge_ref,
    top_ref,
    own_ref,
    rows_ref,
    edge_ref,
    picks_ref,
    traces_ref,
    jump_ref,
    flux_ref,
    coarse_ref,
):
    order_row = order_ref[...]
    keep = kept(order_row)
    start = device_ref[0] * KE
    for c in range(FIELDS):
        coarse = jnp.where(keep, state_ref[c], 0.0)
        coarse_ref[c] = coarse
        rows = exact_dot(trace_ref[...], coarse)
        for f in range(6):
            traces_ref[f, c * QP : (c + 1) * QP, :] = rows[f * QP : (f + 1) * QP, :]
    for f in range(6):
        near = near_ref[f : f + 1, :]
        local = jnp.where(near >= 0, near - start, -(1 << 20))
        at = lax.broadcasted_iota(jnp.int32, (KE, KE), 0)
        own = jnp.where(at == local, 1.0, 0.0).astype(jnp.bfloat16)
        jump_ref[f] = dot_exact(traces_ref[f ^ 1], own) - traces_ref[f]
        if f < 2:
            place = jnp.where(at < HALF, at - HALF, at + HALF)
            picks_ref[f] = jnp.where(place == local, 1.0, 0.0).astype(jnp.bfloat16)
    top = top_ref[...]
    enrich = jnp.where(
        top == 3.0,
        enrich_ref[0],
        jnp.where(top == 4.0, enrich_ref[1], jnp.where(top == 5.0, enrich_ref[2], 0.0)),
    )
    enrich_parts = parts(enrich)
    rows_ref[...] = jnp.zeros(rows_ref.shape, jnp.bfloat16)
    rows_ref[0:RICH, 0:MODES] = enrich_parts[0]
    rows_ref[0:RICH, 128 : 128 + MODES] = enrich_parts[0]
    rows_ref[RICH:, 0:MODES] = enrich_parts[1]
    volume_parts = parts(volume_ref[...])
    new_mask = top == order_row.astype(jnp.float32) + 1.0
    total = jnp.zeros((RICH, KE), jnp.float32)
    for c in range(FIELDS):
        factors = jacobian_ref[c]
        weighted = factors[0:1, :] * coarse_ref[0]
        for h in range(1, FIELDS):
            weighted = weighted + factors[h : h + 1, :] * coarse_ref[h]
        for f in range(6):
            flux = factors[0:1, :] * jump_ref[f, 0:QP, :]
            for h in range(1, FIELDS):
                flux = flux + factors[h : h + 1, :] * jump_ref[f, h * QP : (h + 1) * QP, :]
            flux_ref[f * QP : (f + 1) * QP, :] = flux
        residual = dot_three(volume_parts, weighted) + exact_dot(lift_ref[...], flux_ref[...])
        new = dot_three(enrich_parts, jnp.where(keep, adjoint_ref[c], 0.0))
        new = jnp.where(new_mask, new, 0.0)
        total = total + new * residual
        lifted = exact_dot(lift_edge_ref[...], new)
        for f in range(2):
            for h in range(FIELDS):
                term = factors[h : h + 1, :] * lifted[f * QP : (f + 1) * QP, :]
                rows = slice(h * QP, (h + 1) * QP)
                edge_ref[f, rows, :] = term if c == 0 else edge_ref[f, rows, :] + term
    own_ref[...] = jnp.sum(total, axis=0, keepdims=True)


def own_indicators(device, order_row, near, state, adjoint, jacobian, enrich, volume):
    space = pl.BlockSpec(memory_space=pltpu.VMEM)
    return pl.pallas_call(
        indicator_kernel,
        in_specs=[pl.BlockSpec(memory_space=pltpu.SMEM)] + [space] * 11,
        out_specs=(space,) * 4,
        out_shape=(
            pltpu.HBM((1, KE), jnp.float32),
            pltpu.HBM((2 * RICH, 256), jnp.bfloat16),
            pltpu.HBM((2, FIELDS * QP, KE), jnp.float32),
            pltpu.HBM((2, KE, KE), jnp.bfloat16),
        ),
        scratch_shapes=[
            pltpu.VMEM((6, FIELDS * QP, KE), jnp.float32),
            pltpu.VMEM((6, FIELDS * QP, KE), jnp.float32),
            pltpu.VMEM((6 * QP, KE), jnp.float32),
            pltpu.VMEM((FIELDS, MODES, KE), jnp.float32),
        ],
        compiler_params=pltpu.CompilerParams(vmem_limit_bytes=VMEM),
        name="own_indicators",
    )(
        device,
        order_row,
        near,
        state,
        adjoint,
        jacobian,
        enrich,
        volume,
        jnp.asarray(TRACE, jnp.bfloat16),
        jnp.asarray(LIFT, jnp.bfloat16),
        jnp.asarray(LIFT[:, : 2 * QP].T, jnp.bfloat16),
        jnp.asarray(RICH_TOP),
    )


def unpack_kernel(
    in_ref,
    rows_hbm,
    own_hbm,
    edge_hbm,
    picks_hbm,
    before_hbm,
    after_hbm,
    state_hbm,
    adjoint_hbm,
    ids_hbm,
    orders_hbm,
    indicator_hbm,
    rows_ref,
    own_ref,
    edge_ref,
    picks_ref,
    halo_ref,
    state_ref,
    adjoint_ref,
    ids_ref,
    orders_ref,
    indicator_ref,
    old_ref,
    in_sems,
    out_sems,
):
    loads = [
        pltpu.make_async_copy(rows_hbm, rows_ref, in_sems.at[0]),
        pltpu.make_async_copy(own_hbm, own_ref, in_sems.at[1]),
        pltpu.make_async_copy(edge_hbm, edge_ref, in_sems.at[2]),
        pltpu.make_async_copy(picks_hbm, picks_ref, in_sems.at[3]),
        pltpu.make_async_copy(before_hbm, halo_ref.at[0], in_sems.at[4]),
        pltpu.make_async_copy(after_hbm, halo_ref.at[1], in_sems.at[5]),
    ]
    for copy in loads:
        copy.start()
    slots = ND * CAP
    n = lax.broadcasted_iota(jnp.int32, (RICH, 128), 0)
    i = (n * 57) >> 11
    rest = n - i * 36
    j = (rest * 43) >> 8
    top = jnp.maximum(jnp.maximum(i, j), rest - j * 6)
    top = jnp.concatenate([top] * CAP, axis=1)
    upper = lax.broadcasted_iota(jnp.int32, (ND // 2, 8, 128), 1) >= CAP
    old_ref[...] = jnp.zeros(old_ref.shape, jnp.float32)
    stores = []

    def store(source, target):
        copy = pltpu.make_async_copy(source, target, out_sems.at[len(stores)])
        copy.start()
        stores.append(copy)

    def finish():
        for copy in loads[1:]:
            copy.wait()
        total = own_ref[...]
        for f in range(2):
            halo = jnp.concatenate([halo_ref[0, f ^ 1], halo_ref[1, f ^ 1]], axis=1)
            found = dot_exact(halo, picks_ref[f])
            total = total + jnp.sum(found * edge_ref[f], axis=0, keepdims=True)
        indicator_ref[...] = jnp.abs(total) * (1.0 / 216.0)

    def split(t):
        block = in_ref[:, 8 * t : 8 * t + 8, :].reshape(ND // 2, 2, 8, 128)
        even, odd = block[:, 0], block[:, 1]
        state = jnp.where(upper, pltpu.roll(odd, CAP, 1), even)
        return state, jnp.where(upper, odd, pltpu.roll(even, CAP, 1))

    def put_state(t, state):
        moved = state.reshape(slots, 128).T
        state_ref[t] = moved[0:MODES, :]
        return moved

    def labels(moved):
        id_row = moved[125:126, :].astype(jnp.int32)
        order_row = moved[126:127, :].astype(jnp.int32)
        first = (lax.broadcasted_iota(jnp.int32, (1, slots), 1) >> 2) * KE
        ids_ref[...] = jnp.where(id_row > 0, first + id_row - 1, -1)
        orders_ref[...] = order_row
        return top == order_row + 1

    for t in range(FIELDS):
        moved = put_state(t, split(t)[0])
        if t == 0:
            new_mask = labels(moved)
    store(state_ref, state_hbm)
    loads[0].wait()
    for t in range(FIELDS):
        turned = split(t)[1].reshape(slots, 128).T
        for g in range(25):
            to = 36 * (g // 5) + 6 * (g % 5)
            old_ref[t % 2, to : to + 5, :] = turned[5 * g : 5 * g + 5, :]
        high, low = parts(turned)
        new = dot(rows_ref[0:RICH, :], jnp.concatenate([high, low], axis=0)) + dot(
            rows_ref[RICH:, 0:128], high
        )
        adjoint_ref[t] = jnp.where(new_mask, new, old_ref[t % 2])
        store(adjoint_ref.at[t], adjoint_hbm.at[t])
        if t == 2:
            store(ids_ref, ids_hbm)
            store(orders_ref, orders_hbm)
    finish()
    store(indicator_ref, indicator_hbm)
    for copy in stores:
        copy.wait()


def unpack(received, rows, own, edge, picks, before, after):
    slots = ND * CAP
    far = pl.BlockSpec(memory_space=pltpu.HBM)
    shapes = (
        ((FIELDS, MODES, slots), jnp.float32),
        ((FIELDS, RICH, slots), jnp.float32),
        ((1, slots), jnp.int32),
        ((1, slots), jnp.int32),
        ((1, KE), jnp.float32),
    )
    return pl.pallas_call(
        unpack_kernel,
        in_specs=[pl.BlockSpec(memory_space=pltpu.VMEM)] + [far] * 6,
        out_specs=(far,) * 5,
        out_shape=tuple(pltpu.HBM(*a) for a in shapes),
        scratch_shapes=[
            pltpu.VMEM((2 * RICH, 256), jnp.bfloat16),
            pltpu.VMEM((1, KE), jnp.float32),
            pltpu.VMEM((2, FIELDS * QP, KE), jnp.float32),
            pltpu.VMEM((2, KE, KE), jnp.bfloat16),
            pltpu.VMEM((2, 2, FIELDS * QP, HALF), jnp.float32),
        ]
        + [pltpu.VMEM(*a) for a in shapes]
        + [pltpu.VMEM((2, RICH, slots), jnp.float32)]
        + [pltpu.SemaphoreType.DMA((6,)), pltpu.SemaphoreType.DMA((2 * FIELDS + 3,))],
        compiler_params=pltpu.CompilerParams(vmem_limit_bytes=VMEM),
        name="unpack",
    )(received, hbm(rows), hbm(own), hbm(edge), hbm(picks), hbm(before), hbm(after))


def body(state, adjoint, order, neighbours, owner, jacobian, enrich, volume):
    device = lax.axis_index("dom")
    order_row = order.reshape(1, KE)
    message = pack(order_row, owner.reshape(1, KE), state, adjoint)
    received = lax.all_to_all(message, "dom", split_axis=0, concat_axis=0, tiled=True)
    first, last = edges(order_row, state, jnp.asarray(TRACE, jnp.bfloat16))
    up = [(i, i + 1) for i in range(ND - 1)]
    down = [(i + 1, i) for i in range(ND - 1)]
    before = lax.ppermute(last, "dom", up)
    after = lax.ppermute(first, "dom", down)
    own, rows, edge, picks = own_indicators(
        device.reshape(1), order_row, neighbours, state, adjoint, jacobian, enrich, volume
    )
    moved_state, moved_adjoint, ids, orders, indicator = unpack(
        received, rows, own, edge, picks, before, after
    )
    return (
        indicator.reshape(KE),
        moved_state,
        moved_adjoint,
        ids.reshape(ND * CAP),
        orders.reshape(ND * CAP),
    )


def solution(mesh):
    wide = P(None, None, "dom")
    in_specs = (wide, wide, P("dom"), P(None, "dom"), P("dom", None), wide, P(), P())
    out_specs = (P("dom"), wide, wide, P("dom"), P("dom"))
    return jax.shard_map(body, mesh=mesh, in_specs=in_specs, out_specs=out_specs, check_vma=False)
```

```python
import jax
import jax.numpy as jnp
import numpy as np
from jax import lax
from jax.experimental import pallas as pl
from jax.experimental.pallas import tpu as pltpu
from jax.sharding import PartitionSpec as P

FIELDS = 5
MODES = 125
RICH = 216
PAD = 224
KE = 256
CAP = 4
ND = 128
HALF = 128
QP = 32
LOADS = ((0, 2), (2, 3))
VMEM = 48 * 1024 * 1024


def tables():
    m = np.arange(MODES)
    small = np.stack([m // 25, m // 5 % 5, m % 5])
    n = np.arange(RICH)
    rich = np.stack([n // 36, n // 6 % 6, n % 6])
    trace = np.zeros((6 * QP, MODES), np.float32)
    lift = np.zeros((RICH, 6 * QP), np.float32)
    for f in range(6):
        d = f // 2
        t1, t2 = [a for a in range(3) if a != d]
        s = -1.0 if f % 2 == 0 else 1.0
        trace[f * QP + small[t1] * 5 + small[t2], m] = s ** small[d]
        ok = (rich[t1] < 5) & (rich[t2] < 5)
        weight = s ** rich[d] * (2 * rich[d] + 1) * 0.5
        lift[n[ok], (f * QP + rich[t1] * 5 + rich[t2])[ok]] = weight[ok]
    rich_top = rich.max(axis=0).astype(np.float32)[:, None]
    return trace, lift, rich_top


TRACE, LIFT, RICH_TOP = tables()


def hbm(x):
    return pltpu.with_memory_space_constraint(x, pltpu.HBM)


def dot(a, b):
    return lax.dot_general(a, b, (((1,), (0,)), ((), ())), preferred_element_type=jnp.float32)


def dot_nt(a, b):
    return lax.dot_general(a, b, (((1,), (1,)), ((), ())), preferred_element_type=jnp.float32)


def parts(x):
    high = x.astype(jnp.bfloat16)
    return high, (x - high.astype(jnp.float32)).astype(jnp.bfloat16)


def exact_dot(a, x):
    high, low = parts(x)
    return dot(a, high) + dot(a, low)


def dot_exact(x, a):
    high, low = parts(x)
    return dot(high, a) + dot(low, a)


def dot_three(a, x):
    a_high, a_low = a
    high, low = parts(x)
    return dot(a_high, high) + (dot(a_high, low) + dot(a_low, high))


def kept(order_row):
    m = lax.broadcasted_iota(jnp.int32, (MODES, KE), 0)
    i = (m * 41) >> 10
    rest = m - i * 25
    j = (rest * 13) >> 6
    k = rest - j * 5
    return jnp.maximum(jnp.maximum(i, j), k) <= order_row


def pack_kernel(
    order_hbm,
    owner_hbm,
    state_hbm,
    adjoint_hbm,
    out_hbm,
    order_ref,
    owner_ref,
    state_ref,
    adjoint_ref,
    x_ref,
    out_ref,
    in_sems,
    out_sems,
):
    small = [
        pltpu.make_async_copy(order_hbm, order_ref, in_sems.at[0]),
        pltpu.make_async_copy(owner_hbm, owner_ref, in_sems.at[1]),
    ]
    fields = []
    for first, count in LOADS:
        part = pl.ds(first, count)
        k = len(fields) + 2
        fields.append(pltpu.make_async_copy(state_hbm.at[part], state_ref.at[part], in_sems.at[k]))
        fields.append(
            pltpu.make_async_copy(adjoint_hbm.at[part], adjoint_ref.at[part], in_sems.at[k + 1])
        )
    for copy in small:
        copy.start()
    for copy in fields:
        copy.start()
    before = lax.broadcasted_iota(jnp.int32, (KE, KE), 0) < lax.broadcasted_iota(
        jnp.int32, (KE, KE), 1
    )
    before = jnp.where(before, 1.0, 0.0).astype(jnp.bfloat16)
    local = lax.broadcasted_iota(jnp.int32, (1, KE), 1)
    for t in range(FIELDS):
        x_ref[t, 125:126, :] = (local + 1).astype(jnp.float32)
        x_ref[t, 127:128, :] = jnp.zeros((1, KE), jnp.float32)
        x_ref[t, 253:256, :] = jnp.zeros((3, KE), jnp.float32)
    for copy in small:
        copy.wait()
    order_row = order_ref[...]
    for t in range(FIELDS):
        x_ref[t, 126:127, :] = order_row.astype(jnp.float32)
    hits = owner_ref[...] == lax.broadcasted_iota(jnp.int32, (ND, KE), 0)
    count = dot(jnp.where(hits, 1.0, 0.0).astype(jnp.bfloat16), before)
    rank = jnp.sum(jnp.where(hits, count, 0.0), axis=0, keepdims=True).astype(jnp.int32)
    slot = owner_ref[...] * CAP + rank
    sel = jnp.where(slot == lax.broadcasted_iota(jnp.int32, (CAP * ND, KE), 0), 1.0, 0.0)
    sel = sel.astype(jnp.bfloat16)
    upper = lax.broadcasted_iota(jnp.int32, (ND // 2, 8, 128), 1) >= CAP
    keep = kept(order_row)
    sends = []

    def prepare(t):
        x_ref[t, 0:MODES, :] = jnp.where(keep, state_ref[t], 0.0)
        x_ref[t, 128 : 128 + MODES, :] = jnp.where(keep, adjoint_ref[t], 0.0)
        return parts(x_ref[t])

    def gather(pair):
        return dot_nt(sel, pair[0]) + dot_nt(sel, pair[1])

    def send(t, rows):
        low_rows = rows[:, 0:128].reshape(ND // 2, 8, 128)
        high_rows = rows[:, 128:256].reshape(ND // 2, 8, 128)
        out_ref[t, :, 0] = jnp.where(upper, pltpu.roll(high_rows, CAP, 1), low_rows)
        out_ref[t, :, 1] = jnp.where(upper, high_rows, pltpu.roll(low_rows, CAP, 1))
        copy = pltpu.make_async_copy(
            out_ref.at[t], out_hbm.at[:, :, pl.ds(8 * t, 8), :], out_sems.at[t]
        )
        copy.start()
        sends.append(copy)

    for g, (first, count) in enumerate(LOADS):
        fields[2 * g].wait()
        fields[2 * g + 1].wait()
        for t in range(first, first + count):
            send(t, gather(prepare(t)))
    for copy in sends:
        copy.wait()


def pack(order_row, owner_row, state, adjoint):
    far = pl.BlockSpec(memory_space=pltpu.HBM)
    return pl.pallas_call(
        pack_kernel,
        in_specs=[far] * 4,
        out_specs=far,
        out_shape=pltpu.HBM((ND // 2, 2, 8 * FIELDS, 128), jnp.float32),
        scratch_shapes=[
            pltpu.VMEM((1, KE), jnp.int32),
            pltpu.VMEM((1, KE), jnp.int32),
            pltpu.VMEM((FIELDS, MODES, KE), jnp.float32),
            pltpu.VMEM((FIELDS, MODES, KE), jnp.float32),
            pltpu.VMEM((FIELDS, 256, KE), jnp.float32),
            pltpu.VMEM((FIELDS, ND // 2, 2, 8, 128), jnp.float32),
            pltpu.SemaphoreType.DMA((2 + 2 * len(LOADS),)),
            pltpu.SemaphoreType.DMA((FIELDS,)),
        ],
        compiler_params=pltpu.CompilerParams(vmem_limit_bytes=VMEM),
        name="pack",
    )(hbm(order_row), hbm(owner_row), hbm(state), hbm(adjoint)).reshape(ND, 8 * FIELDS, 128)


def edge_kernel(order_ref, state_ref, trace_ref, first_ref, last_ref):
    keep = kept(order_ref[...])
    for c in range(FIELDS):
        coarse = jnp.where(keep, state_ref[c], 0.0)
        rows = exact_dot(trace_ref[0 : 2 * QP, :], coarse)
        for f in range(2):
            first_ref[f, c * QP : (c + 1) * QP, :] = rows[f * QP : (f + 1) * QP, :HALF]
            last_ref[f, c * QP : (c + 1) * QP, :] = rows[f * QP : (f + 1) * QP, KE - HALF :]


def edges(order_row, state, trace):
    shape = jax.ShapeDtypeStruct((2, FIELDS * QP, HALF), jnp.float32)
    return pl.pallas_call(
        edge_kernel,
        out_shape=(shape, shape),
        compiler_params=pltpu.CompilerParams(vmem_limit_bytes=VMEM),
        name="edges",
    )(order_row, state, trace)


def indicator_kernel(
    device_ref,
    order_ref,
    near_ref,
    state_ref,
    adjoint_ref,
    jacobian_ref,
    enrich_ref,
    volume_ref,
    trace_ref,
    lift_ref,
    lift_edge_ref,
    top_ref,
    own_ref,
    rows_ref,
    edge_ref,
    picks_ref,
    traces_ref,
    jump_ref,
    flux_ref,
    coarse_ref,
):
    order_row = order_ref[...]
    keep = kept(order_row)
    start = device_ref[0] * KE
    for c in range(FIELDS):
        coarse = jnp.where(keep, state_ref[c], 0.0)
        coarse_ref[c] = coarse
        rows = exact_dot(trace_ref[...], coarse)
        for f in range(6):
            traces_ref[f, c * QP : (c + 1) * QP, :] = rows[f * QP : (f + 1) * QP, :]
    for f in range(6):
        near = near_ref[f : f + 1, :]
        local = jnp.where(near >= 0, near - start, -(1 << 20))
        at = lax.broadcasted_iota(jnp.int32, (KE, KE), 0)
        own = jnp.where(at == local, 1.0, 0.0).astype(jnp.bfloat16)
        jump_ref[f] = dot_exact(traces_ref[f ^ 1], own) - traces_ref[f]
        if f < 2:
            place = jnp.where(at < HALF, at - HALF, at + HALF)
            picks_ref[f] = jnp.where(place == local, 1.0, 0.0).astype(jnp.bfloat16)
    top = top_ref[...]
    enrich = jnp.where(
        top == 3.0,
        enrich_ref[0],
        jnp.where(top == 4.0, enrich_ref[1], jnp.where(top == 5.0, enrich_ref[2], 0.0)),
    )
    enrich_parts = parts(enrich)
    padded = jnp.concatenate([enrich, jnp.zeros((PAD - RICH, MODES), jnp.float32)], axis=0)
    high, low = parts(padded)
    rows_ref[...] = jnp.zeros(rows_ref.shape, jnp.bfloat16)
    rows_ref[0:PAD, 0:MODES] = high
    rows_ref[0:PAD, 128 : 128 + MODES] = high
    rows_ref[PAD:, 0:MODES] = low
    volume_parts = parts(volume_ref[...])
    new_mask = top == order_row.astype(jnp.float32) + 1.0
    total = jnp.zeros((RICH, KE), jnp.float32)
    for c in range(FIELDS):
        factors = jacobian_ref[c]
        weighted = factors[0:1, :] * coarse_ref[0]
        for h in range(1, FIELDS):
            weighted = weighted + factors[h : h + 1, :] * coarse_ref[h]
        for f in range(6):
            flux = factors[0:1, :] * jump_ref[f, 0:QP, :]
            for h in range(1, FIELDS):
                flux = flux + factors[h : h + 1, :] * jump_ref[f, h * QP : (h + 1) * QP, :]
            flux_ref[f * QP : (f + 1) * QP, :] = flux
        residual = dot_three(volume_parts, weighted) + exact_dot(lift_ref[...], flux_ref[...])
        new = dot_three(enrich_parts, jnp.where(keep, adjoint_ref[c], 0.0))
        new = jnp.where(new_mask, new, 0.0)
        total = total + new * residual
        lifted = exact_dot(lift_edge_ref[...], new)
        for f in range(2):
            for h in range(FIELDS):
                term = factors[h : h + 1, :] * lifted[f * QP : (f + 1) * QP, :]
                rows = slice(h * QP, (h + 1) * QP)
                edge_ref[f, rows, :] = term if c == 0 else edge_ref[f, rows, :] + term
    own_ref[...] = jnp.sum(total, axis=0, keepdims=True)


def own_indicators(device, order_row, near, state, adjoint, jacobian, enrich, volume):
    space = pl.BlockSpec(memory_space=pltpu.VMEM)
    return pl.pallas_call(
        indicator_kernel,
        in_specs=[pl.BlockSpec(memory_space=pltpu.SMEM)] + [space] * 11,
        out_specs=(space,) * 4,
        out_shape=(
            pltpu.HBM((1, KE), jnp.float32),
            pltpu.HBM((2 * PAD, 256), jnp.bfloat16),
            pltpu.HBM((2, FIELDS * QP, KE), jnp.float32),
            pltpu.HBM((2, KE, KE), jnp.bfloat16),
        ),
        scratch_shapes=[
            pltpu.VMEM((6, FIELDS * QP, KE), jnp.float32),
            pltpu.VMEM((6, FIELDS * QP, KE), jnp.float32),
            pltpu.VMEM((6 * QP, KE), jnp.float32),
            pltpu.VMEM((FIELDS, MODES, KE), jnp.float32),
        ],
        compiler_params=pltpu.CompilerParams(vmem_limit_bytes=VMEM),
        name="own_indicators",
    )(
        device,
        order_row,
        near,
        state,
        adjoint,
        jacobian,
        enrich,
        volume,
        jnp.asarray(TRACE, jnp.bfloat16),
        jnp.asarray(LIFT, jnp.bfloat16),
        jnp.asarray(LIFT[:, : 2 * QP].T, jnp.bfloat16),
        jnp.asarray(RICH_TOP),
    )


def unpack_kernel(
    in_ref,
    rows_hbm,
    own_hbm,
    edge_hbm,
    picks_hbm,
    before_hbm,
    after_hbm,
    state_hbm,
    adjoint_hbm,
    ids_hbm,
    orders_hbm,
    indicator_hbm,
    rows_ref,
    own_ref,
    edge_ref,
    picks_ref,
    halo_ref,
    state_ref,
    adjoint_ref,
    ids_ref,
    orders_ref,
    indicator_ref,
    old_ref,
    in_sems,
    out_sems,
):
    loads = [
        pltpu.make_async_copy(rows_hbm, rows_ref, in_sems.at[0]),
        pltpu.make_async_copy(own_hbm, own_ref, in_sems.at[1]),
        pltpu.make_async_copy(edge_hbm, edge_ref, in_sems.at[2]),
        pltpu.make_async_copy(picks_hbm, picks_ref, in_sems.at[3]),
        pltpu.make_async_copy(before_hbm, halo_ref.at[0], in_sems.at[4]),
        pltpu.make_async_copy(after_hbm, halo_ref.at[1], in_sems.at[5]),
    ]
    for copy in loads:
        copy.start()
    slots = ND * CAP
    n = lax.broadcasted_iota(jnp.int32, (RICH, 128), 0)
    i = (n * 57) >> 11
    rest = n - i * 36
    j = (rest * 43) >> 8
    top = jnp.maximum(jnp.maximum(i, j), rest - j * 6)
    top = jnp.concatenate([top] * CAP, axis=1)
    upper = lax.broadcasted_iota(jnp.int32, (ND // 2, 8, 128), 1) >= CAP
    old_ref[...] = jnp.zeros(old_ref.shape, jnp.float32)
    stores = []

    def store(source, target):
        copy = pltpu.make_async_copy(source, target, out_sems.at[len(stores)])
        copy.start()
        stores.append(copy)

    def finish():
        for copy in loads[1:]:
            copy.wait()
        total = own_ref[...]
        for f in range(2):
            halo = jnp.concatenate([halo_ref[0, f ^ 1], halo_ref[1, f ^ 1]], axis=1)
            found = dot_exact(halo, picks_ref[f])
            total = total + jnp.sum(found * edge_ref[f], axis=0, keepdims=True)
        indicator_ref[...] = jnp.abs(total) * (1.0 / 216.0)

    def split(t):
        block = in_ref[:, 8 * t : 8 * t + 8, :].reshape(ND // 2, 2, 8, 128)
        even, odd = block[:, 0], block[:, 1]
        state = jnp.where(upper, pltpu.roll(odd, CAP, 1), even)
        return state, jnp.where(upper, odd, pltpu.roll(even, CAP, 1))

    def put_state(t, state):
        moved = state.reshape(slots, 128).T
        state_ref[t] = moved[0:MODES, :]
        return moved

    def labels(moved):
        id_row = moved[125:126, :].astype(jnp.int32)
        order_row = moved[126:127, :].astype(jnp.int32)
        first = (lax.broadcasted_iota(jnp.int32, (1, slots), 1) >> 2) * KE
        ids_ref[...] = jnp.where(id_row > 0, first + id_row - 1, -1)
        orders_ref[...] = order_row
        return top == order_row + 1

    for t in range(FIELDS):
        moved = put_state(t, split(t)[0])
        if t == 0:
            new_mask = labels(moved)
    store(state_ref, state_hbm)
    loads[0].wait()
    for t in range(FIELDS):
        turned = split(t)[1].reshape(slots, 128).T
        for g in range(25):
            to = 36 * (g // 5) + 6 * (g % 5)
            old_ref[t % 2, to : to + 5, :] = turned[5 * g : 5 * g + 5, :]
        high, low = parts(turned)
        new = dot(rows_ref[0:PAD, :], jnp.concatenate([high, low], axis=0)) + dot(
            rows_ref[PAD:, 0:128], high
        )
        adjoint_ref[t] = jnp.where(new_mask, new[0:RICH], old_ref[t % 2])
        store(adjoint_ref.at[t], adjoint_hbm.at[t])
        if t == 2:
            store(ids_ref, ids_hbm)
            store(orders_ref, orders_hbm)
    finish()
    store(indicator_ref, indicator_hbm)
    for copy in stores:
        copy.wait()


def unpack(received, rows, own, edge, picks, before, after):
    slots = ND * CAP
    far = pl.BlockSpec(memory_space=pltpu.HBM)
    shapes = (
        ((FIELDS, MODES, slots), jnp.float32),
        ((FIELDS, RICH, slots), jnp.float32),
        ((1, slots), jnp.int32),
        ((1, slots), jnp.int32),
        ((1, KE), jnp.float32),
    )
    return pl.pallas_call(
        unpack_kernel,
        in_specs=[pl.BlockSpec(memory_space=pltpu.VMEM)] + [far] * 6,
        out_specs=(far,) * 5,
        out_shape=tuple(pltpu.HBM(*a) for a in shapes),
        scratch_shapes=[
            pltpu.VMEM((2 * PAD, 256), jnp.bfloat16),
            pltpu.VMEM((1, KE), jnp.float32),
            pltpu.VMEM((2, FIELDS * QP, KE), jnp.float32),
            pltpu.VMEM((2, KE, KE), jnp.bfloat16),
            pltpu.VMEM((2, 2, FIELDS * QP, HALF), jnp.float32),
        ]
        + [pltpu.VMEM(*a) for a in shapes]
        + [pltpu.VMEM((2, RICH, slots), jnp.float32)]
        + [pltpu.SemaphoreType.DMA((6,)), pltpu.SemaphoreType.DMA((2 * FIELDS + 3,))],
        compiler_params=pltpu.CompilerParams(vmem_limit_bytes=VMEM),
        name="unpack",
    )(received, hbm(rows), hbm(own), hbm(edge), hbm(picks), hbm(before), hbm(after))


def body(state, adjoint, order, neighbours, owner, jacobian, enrich, volume):
    device = lax.axis_index("dom")
    order_row = order.reshape(1, KE)
    message = pack(order_row, owner.reshape(1, KE), state, adjoint)
    received = lax.all_to_all(message, "dom", split_axis=0, concat_axis=0, tiled=True)
    first, last = edges(order_row, state, jnp.asarray(TRACE, jnp.bfloat16))
    up = [(i, i + 1) for i in range(ND - 1)]
    down = [(i + 1, i) for i in range(ND - 1)]
    before = lax.ppermute(last, "dom", up)
    after = lax.ppermute(first, "dom", down)
    own, rows, edge, picks = own_indicators(
        device.reshape(1), order_row, neighbours, state, adjoint, jacobian, enrich, volume
    )
    moved_state, moved_adjoint, ids, orders, indicator = unpack(
        received, rows, own, edge, picks, before, after
    )
    return (
        indicator.reshape(KE),
        moved_state,
        moved_adjoint,
        ids.reshape(ND * CAP),
        orders.reshape(ND * CAP),
    )


def solution(mesh):
    wide = P(None, None, "dom")
    in_specs = (wide, wide, P("dom"), P(None, "dom"), P("dom", None), wide, P(), P())
    out_specs = (P("dom"), wide, wide, P("dom"), P("dom"))
    return jax.shard_map(body, mesh=mesh, in_specs=in_specs, out_specs=out_specs, check_vma=False)
```

```python
import jax
import jax.numpy as jnp
import numpy as np
from jax import lax
from jax.experimental import pallas as pl
from jax.experimental.pallas import tpu as pltpu
from jax.sharding import PartitionSpec as P

FIELDS = 5
MODES = 125
RICH = 216
PAD = 224
KE = 256
CAP = 4
ND = 128
HALF = 128
QP = 32
LOADS = ((0, 2), (2, 3))
VMEM = 48 * 1024 * 1024


def tables():
    m = np.arange(MODES)
    small = np.stack([m // 25, m // 5 % 5, m % 5])
    n = np.arange(RICH)
    rich = np.stack([n // 36, n // 6 % 6, n % 6])
    trace = np.zeros((6 * QP, MODES), np.float32)
    lift = np.zeros((RICH, 6 * QP), np.float32)
    for f in range(6):
        d = f // 2
        t1, t2 = [a for a in range(3) if a != d]
        s = -1.0 if f % 2 == 0 else 1.0
        trace[f * QP + small[t1] * 5 + small[t2], m] = s ** small[d]
        ok = (rich[t1] < 5) & (rich[t2] < 5)
        weight = s ** rich[d] * (2 * rich[d] + 1) * 0.5
        lift[n[ok], (f * QP + rich[t1] * 5 + rich[t2])[ok]] = weight[ok]
    rich_top = rich.max(axis=0).astype(np.float32)[:, None]
    return trace, lift, rich_top


TRACE, LIFT, RICH_TOP = tables()


def hbm(x):
    return pltpu.with_memory_space_constraint(x, pltpu.HBM)


def dot(a, b):
    return lax.dot_general(a, b, (((1,), (0,)), ((), ())), preferred_element_type=jnp.float32)


def dot_nt(a, b):
    return lax.dot_general(a, b, (((1,), (1,)), ((), ())), preferred_element_type=jnp.float32)


def parts(x):
    high = x.astype(jnp.bfloat16)
    return high, (x - high.astype(jnp.float32)).astype(jnp.bfloat16)


def exact_dot(a, x):
    high, low = parts(x)
    return dot(a, high) + dot(a, low)


def dot_exact(x, a):
    high, low = parts(x)
    return dot(high, a) + dot(low, a)


def dot_three(a, x):
    a_high, a_low = a
    high, low = parts(x)
    return dot(a_high, high) + (dot(a_high, low) + dot(a_low, high))


def kept(order_row):
    m = lax.broadcasted_iota(jnp.int32, (MODES, KE), 0)
    i = (m * 41) >> 10
    rest = m - i * 25
    j = (rest * 13) >> 6
    k = rest - j * 5
    return jnp.maximum(jnp.maximum(i, j), k) <= order_row


def pack_kernel(
    order_hbm,
    owner_hbm,
    state_hbm,
    adjoint_hbm,
    out_hbm,
    order_ref,
    owner_ref,
    state_ref,
    adjoint_ref,
    x_ref,
    out_ref,
    in_sems,
    out_sems,
):
    small = [
        pltpu.make_async_copy(order_hbm, order_ref, in_sems.at[0]),
        pltpu.make_async_copy(owner_hbm, owner_ref, in_sems.at[1]),
    ]
    fields = []
    for first, count in LOADS:
        part = pl.ds(first, count)
        k = len(fields) + 2
        fields.append(pltpu.make_async_copy(state_hbm.at[part], state_ref.at[part], in_sems.at[k]))
        fields.append(
            pltpu.make_async_copy(adjoint_hbm.at[part], adjoint_ref.at[part], in_sems.at[k + 1])
        )
    for copy in small:
        copy.start()
    for copy in fields:
        copy.start()
    before = lax.broadcasted_iota(jnp.int32, (KE, KE), 0) < lax.broadcasted_iota(
        jnp.int32, (KE, KE), 1
    )
    before = jnp.where(before, 1.0, 0.0).astype(jnp.bfloat16)
    local = lax.broadcasted_iota(jnp.int32, (1, KE), 1)
    for t in range(FIELDS):
        x_ref[t, 125:126, :] = (local + 1).astype(jnp.float32)
        x_ref[t, 127:128, :] = jnp.zeros((1, KE), jnp.float32)
        x_ref[t, 253:256, :] = jnp.zeros((3, KE), jnp.float32)
    for copy in small:
        copy.wait()
    order_row = order_ref[...]
    for t in range(FIELDS):
        x_ref[t, 126:127, :] = order_row.astype(jnp.float32)
    hits = owner_ref[...] == lax.broadcasted_iota(jnp.int32, (ND, KE), 0)
    count = dot(jnp.where(hits, 1.0, 0.0).astype(jnp.bfloat16), before)
    rank = jnp.sum(jnp.where(hits, count, 0.0), axis=0, keepdims=True).astype(jnp.int32)
    slot = owner_ref[...] * CAP + rank
    sel = jnp.where(slot == lax.broadcasted_iota(jnp.int32, (CAP * ND, KE), 0), 1.0, 0.0)
    sel = sel.astype(jnp.bfloat16)
    upper = lax.broadcasted_iota(jnp.int32, (ND // 2, 8, 128), 1) >= CAP
    keep = kept(order_row)
    sends = []

    def prepare(t):
        x_ref[t, 0:MODES, :] = jnp.where(keep, state_ref[t], 0.0)
        x_ref[t, 128 : 128 + MODES, :] = jnp.where(keep, adjoint_ref[t], 0.0)
        return parts(x_ref[t])

    def gather(pair):
        return dot_nt(sel, pair[0]) + dot_nt(sel, pair[1])

    def send(t, rows):
        low_rows = rows[:, 0:128].reshape(ND // 2, 8, 128)
        high_rows = rows[:, 128:256].reshape(ND // 2, 8, 128)
        out_ref[t, :, 0] = jnp.where(upper, pltpu.roll(high_rows, CAP, 1), low_rows)
        out_ref[t, :, 1] = jnp.where(upper, high_rows, pltpu.roll(low_rows, CAP, 1))
        copy = pltpu.make_async_copy(
            out_ref.at[t], out_hbm.at[:, :, pl.ds(8 * t, 8), :], out_sems.at[t]
        )
        copy.start()
        sends.append(copy)

    for g, (first, count) in enumerate(LOADS):
        fields[2 * g].wait()
        fields[2 * g + 1].wait()
        for t in range(first, first + count):
            send(t, gather(prepare(t)))
    for copy in sends:
        copy.wait()


def pack(order_row, owner_row, state, adjoint):
    far = pl.BlockSpec(memory_space=pltpu.HBM)
    return pl.pallas_call(
        pack_kernel,
        in_specs=[far] * 4,
        out_specs=far,
        out_shape=pltpu.HBM((ND // 2, 2, 8 * FIELDS, 128), jnp.float32),
        scratch_shapes=[
            pltpu.VMEM((1, KE), jnp.int32),
            pltpu.VMEM((1, KE), jnp.int32),
            pltpu.VMEM((FIELDS, MODES, KE), jnp.float32),
            pltpu.VMEM((FIELDS, MODES, KE), jnp.float32),
            pltpu.VMEM((FIELDS, 256, KE), jnp.float32),
            pltpu.VMEM((FIELDS, ND // 2, 2, 8, 128), jnp.float32),
            pltpu.SemaphoreType.DMA((2 + 2 * len(LOADS),)),
            pltpu.SemaphoreType.DMA((FIELDS,)),
        ],
        compiler_params=pltpu.CompilerParams(vmem_limit_bytes=VMEM),
        name="pack",
    )(hbm(order_row), hbm(owner_row), hbm(state), hbm(adjoint)).reshape(ND, 8 * FIELDS, 128)


def edge_kernel(order_ref, state_ref, trace_ref, first_ref, last_ref):
    keep = kept(order_ref[...])
    for c in range(FIELDS):
        coarse = jnp.where(keep, state_ref[c], 0.0)
        rows = exact_dot(trace_ref[0 : 2 * QP, :], coarse)
        for f in range(2):
            first_ref[f, c * QP : (c + 1) * QP, :] = rows[f * QP : (f + 1) * QP, :HALF]
            last_ref[f, c * QP : (c + 1) * QP, :] = rows[f * QP : (f + 1) * QP, KE - HALF :]


def edges(order_row, state, trace):
    shape = jax.ShapeDtypeStruct((2, FIELDS * QP, HALF), jnp.float32)
    return pl.pallas_call(
        edge_kernel,
        out_shape=(shape, shape),
        compiler_params=pltpu.CompilerParams(vmem_limit_bytes=VMEM),
        name="edges",
    )(order_row, state, trace)


def indicator_kernel(
    device_ref,
    order_ref,
    near_ref,
    state_ref,
    adjoint_ref,
    jacobian_ref,
    enrich_ref,
    volume_ref,
    trace_ref,
    lift_ref,
    lift_edge_ref,
    top_ref,
    own_ref,
    rows_ref,
    edge_ref,
    picks_ref,
    traces_ref,
    jump_ref,
    flux_ref,
    coarse_ref,
):
    order_row = order_ref[...]
    keep = kept(order_row)
    start = device_ref[0] * KE
    for c in range(FIELDS):
        coarse = jnp.where(keep, state_ref[c], 0.0)
        coarse_ref[c] = coarse
        rows = exact_dot(trace_ref[...], coarse)
        for f in range(6):
            traces_ref[f, c * QP : (c + 1) * QP, :] = rows[f * QP : (f + 1) * QP, :]
    for f in range(6):
        near = near_ref[f : f + 1, :]
        local = jnp.where(near >= 0, near - start, -(1 << 20))
        at = lax.broadcasted_iota(jnp.int32, (KE, KE), 0)
        own = jnp.where(at == local, 1.0, 0.0).astype(jnp.bfloat16)
        jump_ref[f] = dot_exact(traces_ref[f ^ 1], own) - traces_ref[f]
        if f < 2:
            place = jnp.where(at < HALF, at - HALF, at + HALF)
            picks_ref[f] = jnp.where(place == local, 1.0, 0.0).astype(jnp.bfloat16)
    top = top_ref[...]
    enrich = jnp.where(
        top == 3.0,
        enrich_ref[0],
        jnp.where(top == 4.0, enrich_ref[1], jnp.where(top == 5.0, enrich_ref[2], 0.0)),
    )
    enrich_parts = parts(enrich)
    padded = jnp.concatenate([enrich, jnp.zeros((PAD - RICH, MODES), jnp.float32)], axis=0)
    high, low = parts(padded)
    rows_ref[...] = jnp.zeros(rows_ref.shape, jnp.bfloat16)
    rows_ref[0:PAD, 0:MODES] = high
    rows_ref[0:PAD, 128 : 128 + MODES] = high
    rows_ref[PAD:, 0:MODES] = low
    volume_parts = parts(volume_ref[...])
    new_mask = top == order_row.astype(jnp.float32) + 1.0
    total = jnp.zeros((RICH, KE), jnp.float32)
    for c in range(FIELDS):
        factors = jacobian_ref[c]
        weighted = factors[0:1, :] * coarse_ref[0]
        for h in range(1, FIELDS):
            weighted = weighted + factors[h : h + 1, :] * coarse_ref[h]
        for f in range(6):
            flux = factors[0:1, :] * jump_ref[f, 0:QP, :]
            for h in range(1, FIELDS):
                flux = flux + factors[h : h + 1, :] * jump_ref[f, h * QP : (h + 1) * QP, :]
            flux_ref[f * QP : (f + 1) * QP, :] = flux
        residual = dot_three(volume_parts, weighted) + exact_dot(lift_ref[...], flux_ref[...])
        new = dot_three(enrich_parts, jnp.where(keep, adjoint_ref[c], 0.0))
        new = jnp.where(new_mask, new, 0.0)
        total = total + new * residual
        lifted = exact_dot(lift_edge_ref[...], new)
        for f in range(2):
            for h in range(FIELDS):
                term = factors[h : h + 1, :] * lifted[f * QP : (f + 1) * QP, :]
                rows = slice(h * QP, (h + 1) * QP)
                edge_ref[f, rows, :] = term if c == 0 else edge_ref[f, rows, :] + term
    own_ref[...] = jnp.sum(total, axis=0, keepdims=True)


def own_indicators(device, order_row, near, state, adjoint, jacobian, enrich, volume):
    space = pl.BlockSpec(memory_space=pltpu.VMEM)
    return pl.pallas_call(
        indicator_kernel,
        in_specs=[pl.BlockSpec(memory_space=pltpu.SMEM)] + [space] * 11,
        out_specs=(space,) * 4,
        out_shape=(
            pltpu.HBM((1, KE), jnp.float32),
            pltpu.HBM((2 * PAD, 256), jnp.bfloat16),
            pltpu.HBM((2, FIELDS * QP, KE), jnp.float32),
            pltpu.HBM((2, KE, KE), jnp.bfloat16),
        ),
        scratch_shapes=[
            pltpu.VMEM((6, FIELDS * QP, KE), jnp.float32),
            pltpu.VMEM((6, FIELDS * QP, KE), jnp.float32),
            pltpu.VMEM((6 * QP, KE), jnp.float32),
            pltpu.VMEM((FIELDS, MODES, KE), jnp.float32),
        ],
        compiler_params=pltpu.CompilerParams(vmem_limit_bytes=VMEM),
        name="own_indicators",
    )(
        device,
        order_row,
        near,
        state,
        adjoint,
        jacobian,
        enrich,
        volume,
        jnp.asarray(TRACE, jnp.bfloat16),
        jnp.asarray(LIFT, jnp.bfloat16),
        jnp.asarray(LIFT[:, : 2 * QP].T, jnp.bfloat16),
        jnp.asarray(RICH_TOP),
    )


def unpack_kernel(
    in_ref,
    rows_hbm,
    own_hbm,
    edge_hbm,
    picks_hbm,
    before_hbm,
    after_hbm,
    state_hbm,
    adjoint_hbm,
    ids_hbm,
    orders_hbm,
    indicator_hbm,
    rows_ref,
    own_ref,
    edge_ref,
    picks_ref,
    halo_ref,
    state_ref,
    adjoint_ref,
    ids_ref,
    orders_ref,
    indicator_ref,
    old_ref,
    in_sems,
    out_sems,
):
    loads = [
        pltpu.make_async_copy(rows_hbm, rows_ref, in_sems.at[0]),
        pltpu.make_async_copy(own_hbm, own_ref, in_sems.at[1]),
        pltpu.make_async_copy(edge_hbm, edge_ref, in_sems.at[2]),
        pltpu.make_async_copy(picks_hbm, picks_ref, in_sems.at[3]),
        pltpu.make_async_copy(before_hbm, halo_ref.at[0], in_sems.at[4]),
        pltpu.make_async_copy(after_hbm, halo_ref.at[1], in_sems.at[5]),
    ]
    loads[0].start()
    slots = ND * CAP
    n = lax.broadcasted_iota(jnp.int32, (RICH, 128), 0)
    i = (n * 57) >> 11
    rest = n - i * 36
    j = (rest * 43) >> 8
    top = jnp.maximum(jnp.maximum(i, j), rest - j * 6)
    top = jnp.concatenate([top] * CAP, axis=1)
    upper = lax.broadcasted_iota(jnp.int32, (ND // 2, 8, 128), 1) >= CAP
    old_ref[...] = jnp.zeros(old_ref.shape, jnp.float32)
    stores = []

    def store(source, target):
        copy = pltpu.make_async_copy(source, target, out_sems.at[len(stores)])
        copy.start()
        stores.append(copy)

    def finish():
        for copy in loads[1:]:
            copy.wait()
        total = own_ref[...]
        for f in range(2):
            halo = jnp.concatenate([halo_ref[0, f ^ 1], halo_ref[1, f ^ 1]], axis=1)
            found = dot_exact(halo, picks_ref[f])
            total = total + jnp.sum(found * edge_ref[f], axis=0, keepdims=True)
        indicator_ref[...] = jnp.abs(total) * (1.0 / 216.0)

    def split(t):
        block = in_ref[:, 8 * t : 8 * t + 8, :].reshape(ND // 2, 2, 8, 128)
        even, odd = block[:, 0], block[:, 1]
        state = jnp.where(upper, pltpu.roll(odd, CAP, 1), even)
        return state, jnp.where(upper, odd, pltpu.roll(even, CAP, 1))

    def put_state(t, state):
        moved = state.reshape(slots, 128).T
        state_ref[t] = moved[0:MODES, :]
        return moved

    def labels(moved):
        id_row = moved[125:126, :].astype(jnp.int32)
        order_row = moved[126:127, :].astype(jnp.int32)
        first = (lax.broadcasted_iota(jnp.int32, (1, slots), 1) >> 2) * KE
        ids_ref[...] = jnp.where(id_row > 0, first + id_row - 1, -1)
        orders_ref[...] = order_row
        return top == order_row + 1

    for t in range(FIELDS):
        moved = put_state(t, split(t)[0])
        if t == 0:
            new_mask = labels(moved)
    store(state_ref, state_hbm)
    for copy in loads[1:]:
        copy.start()
    loads[0].wait()
    for t in range(FIELDS):
        turned = split(t)[1].reshape(slots, 128).T
        for g in range(25):
            to = 36 * (g // 5) + 6 * (g % 5)
            old_ref[t % 2, to : to + 5, :] = turned[5 * g : 5 * g + 5, :]
        high, low = parts(turned)
        new = dot(rows_ref[0:PAD, :], jnp.concatenate([high, low], axis=0)) + dot(
            rows_ref[PAD:, 0:128], high
        )
        adjoint_ref[t] = jnp.where(new_mask, new[0:RICH], old_ref[t % 2])
        store(adjoint_ref.at[t], adjoint_hbm.at[t])
        if t == 2:
            store(ids_ref, ids_hbm)
            store(orders_ref, orders_hbm)
    finish()
    store(indicator_ref, indicator_hbm)
    for copy in stores:
        copy.wait()


def unpack(received, rows, own, edge, picks, before, after):
    slots = ND * CAP
    far = pl.BlockSpec(memory_space=pltpu.HBM)
    shapes = (
        ((FIELDS, MODES, slots), jnp.float32),
        ((FIELDS, RICH, slots), jnp.float32),
        ((1, slots), jnp.int32),
        ((1, slots), jnp.int32),
        ((1, KE), jnp.float32),
    )
    return pl.pallas_call(
        unpack_kernel,
        in_specs=[pl.BlockSpec(memory_space=pltpu.VMEM)] + [far] * 6,
        out_specs=(far,) * 5,
        out_shape=tuple(pltpu.HBM(*a) for a in shapes),
        scratch_shapes=[
            pltpu.VMEM((2 * PAD, 256), jnp.bfloat16),
            pltpu.VMEM((1, KE), jnp.float32),
            pltpu.VMEM((2, FIELDS * QP, KE), jnp.float32),
            pltpu.VMEM((2, KE, KE), jnp.bfloat16),
            pltpu.VMEM((2, 2, FIELDS * QP, HALF), jnp.float32),
        ]
        + [pltpu.VMEM(*a) for a in shapes]
        + [pltpu.VMEM((2, RICH, slots), jnp.float32)]
        + [pltpu.SemaphoreType.DMA((6,)), pltpu.SemaphoreType.DMA((2 * FIELDS + 3,))],
        compiler_params=pltpu.CompilerParams(vmem_limit_bytes=VMEM),
        name="unpack",
    )(received, hbm(rows), hbm(own), hbm(edge), hbm(picks), hbm(before), hbm(after))


def body(state, adjoint, order, neighbours, owner, jacobian, enrich, volume):
    device = lax.axis_index("dom")
    order_row = order.reshape(1, KE)
    message = pack(order_row, owner.reshape(1, KE), state, adjoint)
    received = lax.all_to_all(message, "dom", split_axis=0, concat_axis=0, tiled=True)
    first, last = edges(order_row, state, jnp.asarray(TRACE, jnp.bfloat16))
    up = [(i, i + 1) for i in range(ND - 1)]
    down = [(i + 1, i) for i in range(ND - 1)]
    before = lax.ppermute(last, "dom", up)
    after = lax.ppermute(first, "dom", down)
    own, rows, edge, picks = own_indicators(
        device.reshape(1), order_row, neighbours, state, adjoint, jacobian, enrich, volume
    )
    moved_state, moved_adjoint, ids, orders, indicator = unpack(
        received, rows, own, edge, picks, before, after
    )
    return (
        indicator.reshape(KE),
        moved_state,
        moved_adjoint,
        ids.reshape(ND * CAP),
        orders.reshape(ND * CAP),
    )


def solution(mesh):
    wide = P(None, None, "dom")
    in_specs = (wide, wide, P("dom"), P(None, "dom"), P("dom", None), wide, P(), P())
    out_specs = (P("dom"), wide, wide, P("dom"), P("dom"))
    return jax.shard_map(body, mesh=mesh, in_specs=in_specs, out_specs=out_specs, check_vma=False)
```
